256 devices in a mesh: ex: 2 (over x_hi), ey: 2 (over x_lo), lin: 64 (over z, y, core).
Axes of the slice: x: 4 (x_hi: 2, x_lo: 2; x = x_hi * 2 + x_lo), y: 4, z: 8, core: 2. Of those that a mesh axis runs over, the one named last changes fastest.
Arguments:
- load: float32 [5, 5, 5, 4, 128, 256], P(None, None, None, None, ('ey', 'lin'), 'ex'), may hold values from -6 to 6
- kappa: float32 [4, 128, 256], P(None, ('ey', 'lin'), 'ex'), may hold values from 0.3 to 3
- wet: int32 [4, 128, 256], P(None, ('ey', 'lin'), 'ex'), may hold values 0 or 1
Outputs:
- solution: float32 [5, 5, 5, 4, 128, 256], P(None, None, None, None, ('ey', 'lin'), 'ex')
- residual: float32 [5, 5, 5, 4, 128, 256], P(None, None, None, None, ('ey', 'lin'), 'ex')
The draws below stay inside these ranges and needn't reach their ends.
All inputs are finite; a program needn't handle non-finite values. No bound on the sum of `wet` on one device may be relied on, other than what follows from the above.
Results may differ from the reference program's by a relative error of at most 0.00016.
Values sent between devices are 32-bit elements; how exact they have to be, the bound alone decides.
No kernel may reach another device: no remote copies, remote signals or barrier semaphores. Data moves between devices by JAX's collectives and lax.ppermute only.
A program may use at most 64 MiB of HBM per device.

```python
import math
import jax
import jax.numpy as jnp
import numpy as np
from jax import lax

LOBATTO_NODES = 5
ELEMENTS_DEPTH = 4
CYCLES = 2
NPRE = 2
NPOST = 2
NC = 4
ELEMENTS_ALONG = 256
ELEMENTS_ACROSS = 128


def set_ends(values, stream_key, low, top_value):
    shape = values.shape
    index_at = [jax.random.randint(jax.random.fold_in(stream_key, axis), (), 0, shape[axis]) for axis in range(len(shape))]
    values = values.at[tuple(index_at)].set(low)
    longest = shape.index(max(shape))
    index_at[longest] = (index_at[longest] + 1) % shape[longest]
    return values.at[tuple(index_at)].set(top_value)


def block_scale(key, extent, split, low, top_value):
    level, own = 1.0, jax.random.fold_in(key, 6)
    for position, shards_of in split:
        steps = jnp.exp(jax.random.uniform(jax.random.fold_in(own, position), (shards_of,), jnp.float32, low / len(split), top_value / len(split)))
        level = level * jnp.repeat(steps, extent[position] // shards_of).reshape([-1 if axis == position else 1 for axis in range(len(extent))])
    return level


def scatter_about(own_key, dims, deviation, bound, shards=(), kind=jnp.bfloat16):
    values = jax.random.normal(own_key, dims, jnp.float32) * deviation
    if len(shards) > 0:
        values = block_scale(own_key, dims, shards, -0.22, 0.18) * values
    return jnp.clip(values, min=-bound, max=bound).astype(kind)


def setup_inputs(seed: int = 0) -> dict:
    splits = jax.random.split(jax.random.key(seed), 4)
    load = scatter_about(splits[0], (LOBATTO_NODES, LOBATTO_NODES, LOBATTO_NODES, ELEMENTS_DEPTH, ELEMENTS_ACROSS, ELEMENTS_ALONG), 1.0, 6.0, ((4, 128), (5, 2)), jnp.float32)
    kappa = jnp.clip(jnp.exp(math.log(3.0) - 2.3025851 * jax.random.uniform(splits[1], (ELEMENTS_DEPTH, ELEMENTS_ACROSS, ELEMENTS_ALONG), jnp.float32) ** block_scale(splits[1], (ELEMENTS_DEPTH, ELEMENTS_ACROSS, ELEMENTS_ALONG), ((1, 128), (2, 2)), -0.2, 0.2)), 0.3, 3.0)
    wet = set_ends((jax.random.randint(splits[2], (ELEMENTS_DEPTH, ELEMENTS_ACROSS, ELEMENTS_ALONG), 0, 4) < 3).astype(jnp.int32), jax.random.fold_in(splits[2], 1), 0, 1)
    return dict(load=load, kappa=kappa, wet=wet)


fine_relax = 0.25
coarse_relax = 0.4

def node_tables():
    points = np.array([-1.0, -math.sqrt(3.0 / 7.0), 0.0, math.sqrt(3.0 / 7.0), 1.0])
    weights = np.array([0.1, 49.0 / 90.0, 32.0 / 45.0, 49.0 / 90.0, 0.1])
    eye_table = np.eye(points.shape[0])
    spread = points[:, None] - points[None, :] + eye_table
    factors = np.prod(spread, axis=1)
    deriv = factors[:, None] / (factors[None, :] * spread)
    deriv = np.where(eye_table > 0, (np.sum(1.0 / spread, axis=1) - 1.0)[:, None], deriv)
    stiff = deriv.T @ (weights[:, None] * deriv)
    mass = eye_table * weights[:, None]
    interp = np.stack([(1.0 - points) / 2.0, (1.0 + points) / 2.0], axis=1)
    coarse_stiff = interp.T @ stiff @ interp
    coarse_mass = interp.T @ mass @ interp
    return [jnp.asarray(table, jnp.float32) for table in (stiff, mass, interp, coarse_stiff, coarse_mass)]

def along(matrix, field, axis):
    if axis == 0:
        return jnp.einsum('pa,a...->p...', matrix, field, precision=lax.Precision.HIGHEST)
    if axis == 1:
        return jnp.einsum('qb,ab...->aq...', matrix, field, precision=lax.Precision.HIGHEST)
    return jnp.einsum('rc,abc...->abr...', matrix, field, precision=lax.Precision.HIGHEST)

def element_apply(field, coeff, stiff, mass):
    mass_c = along(mass, field, 2)
    mass_bc = along(mass, mass_c, 1)
    first_term = along(stiff, mass_bc, 0)
    second_term = along(mass, along(stiff, mass_c, 1), 0)
    third_term = along(mass, along(mass, along(stiff, field, 2), 1), 0)
    return coeff * (first_term + second_term + third_term)

def element_diagonal(coeff, stiff, mass):
    stiff_diag = jnp.diagonal(stiff)
    mass_diag = jnp.diagonal(mass)
    local = stiff_diag[:, None, None] * mass_diag[None, :, None] * mass_diag[None, None, :] + mass_diag[:, None, None] * stiff_diag[None, :, None] * mass_diag[None, None, :] + mass_diag[:, None, None] * mass_diag[None, :, None] * stiff_diag[None, None, :]
    return local[:, :, :, None, None, None] * coeff[None, None, None]

def pair_sum(field, node_axis, fetch):
    count = field.shape[node_axis]
    lower = lax.index_in_dim(field, 0, node_axis, keepdims=False)
    upper = lax.index_in_dim(field, count - 1, node_axis, keepdims=False)
    elem_axis = node_axis + 2
    length = lower.shape[elem_axis]
    lower_first = lax.slice_in_dim(lower, 0, 1, axis=elem_axis)
    upper_last = lax.slice_in_dim(upper, length - 1, length, axis=elem_axis)
    outer = fetch(jnp.concatenate([lower_first, upper_last], axis=elem_axis))
    inner = lax.slice_in_dim(upper, 0, length - 1, axis=elem_axis) + lax.slice_in_dim(lower, 1, length, axis=elem_axis)
    head = lower_first + lax.slice_in_dim(outer, 0, 1, axis=elem_axis)
    tail = upper_last + lax.slice_in_dim(outer, 3, 4, axis=elem_axis)
    new_lower = jnp.concatenate([head, inner], axis=elem_axis)
    new_upper = jnp.concatenate([inner, tail], axis=elem_axis)
    middle = lax.slice_in_dim(field, 1, count - 1, axis=node_axis)
    return jnp.concatenate([jnp.expand_dims(new_lower, node_axis), middle, jnp.expand_dims(new_upper, node_axis)], axis=node_axis)

def pad_edge(axis):

    def padded(edge):
        widths = [(1, 1) if dim == axis else (0, 0) for dim in range(edge.ndim)]
        return jnp.pad(edge, widths)
    return padded

def assemble(field, fetch_x, fetch_y, fetch_z):
    field = pair_sum(field, 2, fetch_x)
    field = pair_sum(field, 1, fetch_y)
    return pair_sum(field, 0, fetch_z)

def surface_mask(count, layers, offset, total):
    node = jnp.arange(count, dtype=jnp.int32)[:, None]
    layer = jnp.arange(layers, dtype=jnp.int32)[None, :] + offset
    keep = jnp.where((node == count - 1) & (layer == total - 1), jnp.float32(0.0), jnp.float32(1.0))
    return keep.reshape(count, 1, 1, layers, 1, 1)

def coarse_sweeps(local, coeff, coarse_sum, keep, inverse, coarse_stiff, coarse_mass):
    restricted = keep * coarse_sum(local)
    correction = inverse * restricted
    for sweep in range(NC - 1):
        image = keep * coarse_sum(element_apply(correction, coeff, coarse_stiff, coarse_mass))
        correction = correction + inverse * (restricted - image)
    return correction

def multigrid(load, coeff, fine_sum, keep, coarse_correct, tables):
    stiff, mass, interp, coarse_stiff, coarse_mass = tables
    inverse = fine_relax / fine_sum(element_diagonal(coeff, stiff, mass))
    rhs = keep * fine_sum(load)
    solution = jnp.zeros_like(load)

    def sweep_once(solution):
        change = keep * fine_sum(load - element_apply(solution, coeff, stiff, mass))
        return solution + inverse * change
    transpose = interp.T
    for cycle in range(CYCLES):
        for sweep in range(NPRE):
            if cycle == 0 and sweep == 0:
                solution = solution + inverse * rhs
            else:
                solution = sweep_once(solution)
        local = load - element_apply(solution, coeff, stiff, mass)
        local = along(transpose, along(transpose, along(transpose, local, 2), 1), 0)
        correction = coarse_correct(local)
        solution = solution + along(interp, along(interp, along(interp, correction, 2), 1), 0)
        for sweep in range(NPOST):
            solution = sweep_once(solution)
    residual = keep * fine_sum(load - element_apply(solution, coeff, stiff, mass))
    return (solution, residual)

def reference(load, kappa, wet):
    tables = node_tables()
    stiff, mass, interp, coarse_stiff, coarse_mass = tables
    coeff = kappa * jnp.where(wet == 1, jnp.float32(1.0), jnp.float32(0.05))

    def whole_sum(field):
        return assemble(field, pad_edge(4), pad_edge(3), pad_edge(2))
    fine_retain_mask = surface_mask(LOBATTO_NODES, ELEMENTS_DEPTH, 0, ELEMENTS_DEPTH)
    coarse_retain_mask = surface_mask(2, ELEMENTS_DEPTH, 0, ELEMENTS_DEPTH)
    coarse_inverse = coarse_relax / whole_sum(element_diagonal(coeff, coarse_stiff, coarse_mass))

    def coarse_correct(local):
        return coarse_sweeps(local, coeff, whole_sum, coarse_retain_mask, coarse_inverse, coarse_stiff, coarse_mass)
    return multigrid(load, coeff, whole_sum, fine_retain_mask, coarse_correct, tables)
```

```python
import math

import jax
import jax.numpy as jnp
import numpy as np
from jax import lax
from jax.experimental import pallas as pl
from jax.experimental.pallas import tpu as pltpu
from jax.sharding import PartitionSpec as P

AXES = ("ex", "ey", "lin")
N = 5
NC = 4
WIN = 14
FINE_RELAX = 0.25
COARSE_RELAX = 0.4
F32 = jnp.float32

points = np.array([-1.0, -math.sqrt(3.0 / 7.0), 0.0, math.sqrt(3.0 / 7.0), 1.0])
weights = np.array([0.1, 49.0 / 90.0, 32.0 / 45.0, 49.0 / 90.0, 0.1])


def stiffness():
    eye = np.eye(N)
    spread = points[:, None] - points[None, :] + eye
    factors = np.prod(spread, axis=1)
    deriv = factors[:, None] / (factors[None, :] * spread)
    deriv = np.where(eye > 0, (np.sum(1.0 / spread, axis=1) - 1.0)[:, None], deriv)
    return deriv.T @ (weights[:, None] * deriv)


STIFF = stiffness()
LINE = STIFF / weights[:, None]
EVEN = [[float(LINE[i, j] + LINE[i, 4 - j]) / 2 for j in range(2)] for i in range(3)]
ODD = [[float(LINE[i, j] - LINE[i, 4 - j]) / 2 for j in range(2)] for i in range(2)]
INTERP = np.stack([(1.0 - points) / 2.0, (1.0 + points) / 2.0], axis=1)
SYM = [0, 1, 2, 1, 0]


def weight(*nodes):
    return float(np.prod([weights[SYM[k]] for k in sorted(SYM[n] for n in nodes)]))


def inverse_factor(a, b, c):
    s, w = np.diag(STIFF), weights
    a, b, c = sorted(SYM[n] for n in (a, b, c))
    return FINE_RELAX / float(s[a] * w[b] * w[c] + w[a] * s[b] * w[c] + w[a] * w[b] * s[c])


def at(a, b, c):
    return a * 25 + b * 5 + c


def line(u):
    m2 = u[2] + u[2]
    e0, e1 = u[0] + u[4] - m2, u[1] + u[3] - m2
    o0, o1 = u[0] - u[4], u[1] - u[3]
    even = [EVEN[i][0] * e0 + EVEN[i][1] * e1 for i in range(3)]
    odd = [ODD[i][0] * o0 + ODD[i][1] * o1 for i in range(2)]
    return [even[0] + odd[0], even[1] + odd[1], even[2], even[1] - odd[1], even[0] - odd[0]]


class Moves:
    def __init__(self, info=None):
        sub = lax.broadcasted_iota(jnp.int32, (8, 128), 0)
        lane = lax.broadcasted_iota(jnp.int32, (8, 128), 1)
        self.low = sub < 4
        self.top = (sub & 3) == 3
        self.bottom = (sub & 3) == 0
        self.lane_first = lane == 0
        self.lane_last = lane == 127
        self.last = jnp.logical_and(lane == 127, sub >= 4)
        if info is not None:
            self.even = jnp.full((8, 128), info[0], jnp.int32) == 0
            self.copy0 = jnp.full((8, 128), info[1], jnp.int32) == 0
            self.strip = info[2]

    def above(self, x):
        return jnp.where(self.top, 0.0, pltpu.roll(x, 7, 0))

    def below(self, x):
        return jnp.where(self.bottom, 0.0, pltpu.roll(x, 1, 0))

    def before(self, x):
        r = pltpu.roll(x, 1, 1)
        return jnp.where(self.lane_first, jnp.where(self.low, 0.0, pltpu.roll(r, 4, 0)), r)

    def after(self, x, end):
        r = pltpu.roll(x, 127, 1)
        return jnp.where(self.lane_last, jnp.where(self.low, pltpu.roll(r, 4, 0), end), r)

    def pick(self, x, y):
        return jnp.where(self.even, x, y)


def apply_operator(mv, u_ref, coeff, y_ref, acc_ref, up_ref):
    for b in range(N):
        for c in range(N):
            u = [u_ref[at(a, b, c)] for a in range(4)]
            u.append(mv.above(u[0]))
            up_ref[b * 5 + c] = u[4]
            for a, value in enumerate(line(u)):
                acc_ref[at(a, b, c)] = value
    for a in (4, 0, 1, 2, 3):
        scale = {}
        for b in range(3):
            for c in range(b, 3):
                scale[b, c] = scale[c, b] = coeff * weight(a, b, c)
        u = [[up_ref[b * 5 + c] if a == 4 else u_ref[at(a, b, c)] for c in range(N)] for b in range(N)]
        across = [line([u[b][c] for b in range(N)]) for c in range(N)]
        for b in range(N):
            along = line(u[b])
            y = [(acc_ref[at(a, b, c)] + along[c] + across[c][b]) * scale[SYM[b], SYM[c]] for c in range(N)]
            if a == 4:
                for c in range(N):
                    up_ref[b * 5 + c] = y[c]
                continue
            if a == 0:
                y = [y[c] + mv.below(up_ref[b * 5 + c]) for c in range(N)]
            y[0] = y[0] + mv.before(y[4])
            for c in range(N):
                y_ref[at(a, b, c)] = y[c]


def put_faces(mv, y_ref, a_ref, b_ref, first=0):
    for a in range(4):
        for c in range(N):
            low, high = y_ref[at(a, 0, c)], y_ref[at(a, 4, c)]
            a_ref[first + a * 5 + c] = mv.pick(high, low)
            b_ref[first + a * 5 + c] = mv.pick(low, high)


def got_faces(mv, a_ref, b_ref, count, strips, a_first=0, b_first=0):
    has_left = jnp.where(mv.strip > 0, 1.0, 0.0).astype(F32)
    has_right = jnp.where(mv.strip < strips - 1, 1.0, 0.0).astype(F32)
    left, right = [], []
    for k in range(count):
        x, y = a_ref[a_first + k], b_ref[b_first + k]
        left.append(mv.pick(y, x) * has_left)
        right.append(mv.pick(x, y) * has_right)
    return left, right


def inverse_at(inv_ref, a, b, c):
    kind = (0 if a == 0 else 6) + (0 if b == 0 else 4 if b == 4 else 2) + (0 if c == 0 else 1)
    return inv_ref[kind] * inverse_factor(a, b, c)


def residual_row(mv, f_ref, y_ref, left, right, a, b):
    row = []
    for c in range(N):
        r = f_ref[at(a, b, c)] - y_ref[at(a, b, c)]
        if b == 0:
            r = r - left[a * 5 + c]
        if b == 4:
            r = r - right[a * 5 + c]
        row.append(r)
    return row


def smooth(mv, u_ref, f_ref, y_ref, left, right, inv_ref, out_ref):
    for a in range(4):
        for b in range(N):
            r = residual_row(mv, f_ref, y_ref, left, right, a, b)
            u = [u_ref[at(a, b, c)] + r[c] * inverse_at(inv_ref, a, b, c) for c in range(N)]
            u[4] = mv.after(u[0], u[4])
            for c in range(N):
                out_ref[at(a, b, c)] = u[c]


def half_rows(mv, ref, out_ref):
    for n in range(0, 100, 2):
        x, y = ref[n], ref[n + 1]
        x = jnp.where(mv.copy0, x, pltpu.roll(x, 4, 0))
        y = jnp.where(mv.copy0, pltpu.roll(y, 4, 0), y)
        out_ref[pl.ds(4 * n, 8)] = jnp.where(mv.low, x, y)


def pack_kernel(load_ref, kappa_ref, wet_ref, out_ref):
    row = lax.broadcasted_iota(jnp.int32, (100, 128), 0)
    out_ref[pl.ds(0, 100)] = load_ref[pl.ds(0, 100)] + jnp.where((row & 3) == 0, 0.0, load_ref[pl.ds(399, 100)])
    out_ref[pl.ds(100, 300)] = load_ref[pl.ds(100, 300)]
    coeff = kappa_ref[...] * jnp.where(wet_ref[...] == 1, 1.0, 0.05).astype(F32)
    out_ref[pl.ds(400, 4)] = coeff
    out_ref[pl.ds(404, 4)] = coeff


def unpack_kernel(info, same_ref, other_ref, f_ref, coeff_ref, a_ref, b_ref):
    mv = Moves(info)

    def pair(n):
        x, y = same_ref[pl.ds(4 * n, 8)], other_ref[pl.ds(4 * n, 8)]
        h0, h1 = jnp.where(mv.copy0, x, y), jnp.where(mv.copy0, y, x)
        return jnp.where(mv.low, h0, pltpu.roll(h1, 4, 0)), jnp.where(mv.low, pltpu.roll(h0, 4, 0), h1)

    for n in range(0, 100, 2):
        f_ref[n], f_ref[n + 1] = pair(n)
    coeff, _ = pair(100)
    coeff_ref[...] = coeff
    for a in range(4):
        for b in range(N):
            f_ref[at(a, b, 0)] = f_ref[at(a, b, 0)] + mv.before(f_ref[at(a, b, 4)])
    put_faces(mv, f_ref, a_ref, b_ref)
    a_ref[20] = coeff
    b_ref[20] = coeff


def first_kernel(strips, info, part_ref, coeff_ref, ga_ref, gb_ref, u_ref, y_ref, f_ref, inv_ref, a_ref, b_ref, acc_ref, up_ref):
    mv = Moves(info)
    left, right = got_faces(mv, ga_ref, gb_ref, 21, strips)
    coeff = coeff_ref[...]
    for kind_b, value in enumerate((coeff + left[20], coeff, coeff + right[20])):
        for kind_a, v in enumerate((value + mv.below(value), value)):
            inv_ref[kind_a * 6 + kind_b * 2] = 1.0 / (v + mv.before(v))
            inv_ref[kind_a * 6 + kind_b * 2 + 1] = 1.0 / v
    for a in range(4):
        for b in range(N):
            f = [part_ref[at(a, b, c)] for c in range(N)]
            if b == 0:
                f = [f[c] + left[a * 5 + c] for c in range(N)]
            if b == 4:
                f = [f[c] + right[a * 5 + c] for c in range(N)]
            u = [f[c] * inverse_at(inv_ref, a, b, c) for c in range(N)]
            u[4] = mv.after(u[0], u[4])
            for c in range(N):
                f_ref[at(a, b, c)] = f[c]
                u_ref[at(a, b, c)] = u[c]
    apply_operator(mv, u_ref, coeff, y_ref, acc_ref, up_ref)
    put_faces(mv, y_ref, a_ref, b_ref)


def sweep_kernel(strips, info, u_ref, y_ref, f_ref, inv_ref, coeff_ref, ga_ref, gb_ref, un_ref, yn_ref, a_ref, b_ref, acc_ref, up_ref):
    mv = Moves(info)
    left, right = got_faces(mv, ga_ref, gb_ref, 20, strips)
    smooth(mv, u_ref, f_ref, y_ref, left, right, inv_ref, un_ref)
    apply_operator(mv, un_ref, coeff_ref[...], yn_ref, acc_ref, up_ref)
    put_faces(mv, yn_ref, a_ref, b_ref)


def last_sweep_kernel(strips, info, u_ref, y_ref, f_ref, inv_ref, coeff_ref, ga_ref, gb_ref, yn_ref, a_ref, b_ref, half_ref, un_ref, acc_ref, up_ref):
    sweep_kernel(strips, info, u_ref, y_ref, f_ref, inv_ref, coeff_ref, ga_ref, gb_ref, un_ref, yn_ref, a_ref, b_ref, acc_ref, up_ref)
    half_rows(Moves(info), un_ref, half_ref)


def restrict_kernel(strips, info, u_ref, y_ref, f_ref, inv_ref, coeff_ref, ga_ref, gb_ref, part_ref, un_ref, own_ref, a_ref, b_ref, yn_ref, acc_ref, up_ref):
    mv = Moves(info)
    left, right = got_faces(mv, ga_ref, gb_ref, 20, strips)
    smooth(mv, u_ref, f_ref, y_ref, left, right, inv_ref, un_ref)
    apply_operator(mv, un_ref, coeff_ref[...], yn_ref, acc_ref, up_ref)
    put_faces(mv, yn_ref, a_ref, b_ref, 5)
    z = [[], []]
    for c in range(N):
        rows = [[], []]
        for a in range(4):
            r = [part_ref[at(a, b, c)] - yn_ref[at(a, b, c)] for b in range(N)]
            inner = [sum(float(INTERP[b, side]) * r[b] for b in (1, 2, 3)) for side in range(2)]
            rows[0].append(r[0] + inner[0])
            rows[1].append(r[4] + inner[1])
        for side in range(2):
            x = rows[side]
            low = x[0] + sum(float(INTERP[a, 0]) * x[a] for a in (1, 2, 3))
            z[side].append(low + mv.below(sum(float(INTERP[a, 1]) * x[a] for a in (1, 2, 3))))
    for side in range(2):
        x = z[side]
        inner = [sum(float(INTERP[c, k]) * x[c] for c in (1, 2, 3)) for k in range(2)]
        own_ref[side * 2] = x[0] + inner[0] + mv.before(inner[1])
        own_ref[side * 2 + 1] = jnp.where(mv.last, x[4] + inner[1], 0.0)
    own_ref[4] = coeff_ref[...]
    for k in range(5):
        a_ref[k] = own_ref[k]


def chip_kernel(info, own_ref, ga_ref, b_ref, chip_ref, near_ref):
    mv = Moves(info)
    for k in range(5):
        x, y = own_ref[k], ga_ref[k]
        low, high = mv.pick(x, y), mv.pick(y, x)
        chip_ref[k] = low
        chip_ref[5 + k] = high
        near_ref[k] = low
        near_ref[5 + k] = high
    for k in range(20):
        near_ref[10 + k] = b_ref[5 + k]


def side_kernel(near_ref, second_ref, third_ref, out_ref):
    for k in range(10):
        out_ref[k] = near_ref[k]
        out_ref[10 + k] = second_ref[k]
        out_ref[20 + k] = third_ref[k]


def coarse_solve(mv, strips, chip_ref, mine_ref, other_ref):
    base = mv.strip - (mv.strip & 1) - 6
    window = []
    for w in range(WIN):
        rows = []
        ok = jnp.where(jnp.logical_and(base + w >= 0, base + w < strips), 1.0, 0.0).astype(F32)
        for k in range(5):
            if w in (6, 7):
                rows.append(chip_ref[(w - 6) * 5 + k])
                continue
            if w < 6:
                slot = (2 - w // 2) * 10 + (w % 2) * 5 + k
                x = mv.pick(mine_ref[slot], other_ref[slot])
            else:
                slot = (w // 2 - 4) * 10 + (w % 2) * 5 + k
                x = mv.pick(other_ref[slot], mine_ref[slot])
            rows.append(x * ok)
        window.append(rows)
    coeffs = [rows[4] for rows in window]
    load, inverse, value = {}, {}, {}
    factor = COARSE_RELAX / (2.0 / 3.0)
    for j in range(2, 13):
        load[j] = [window[j - 1][2 + g] + window[j][g] for g in range(2)]
        k = coeffs[j - 1] + coeffs[j]
        k = k + mv.below(k)
        inverse[j] = [jnp.where(v > 0.0, factor / v, 0.0) for v in (k + mv.before(k), k)]
        value[j] = [inverse[j][g] * load[j][g] for g in range(2)]
    for step in range(NC - 1):
        first, final = 2 + step, 12 - step
        nodes = {}
        for j in range(first, final + 1):
            value[j][1] = mv.after(value[j][0], value[j][1])
            nodes[j] = [value[j], [mv.above(v) for v in value[j]]]
        sums = {j: [[None, None], [None, None]] for j in range(first, final + 1)}
        for j in range(first, final):
            v = {(a, b, c): nodes[j + b][a][c] for a in range(2) for b in range(2) for c in range(2)}
            for axis in range(3):
                v = butterfly(v, axis)
            cf = [coeffs[j] * 0.125, coeffs[j] * (0.125 * 2.0 / 3.0), coeffs[j] * (0.125 / 3.0)]
            v = {key: None if sum(key) == 0 else x * cf[sum(key) - 1] for key, x in v.items()}
            for axis in range(3):
                v = butterfly(v, axis)
            for (a, b, c), x in v.items():
                old = sums[j + b][a][c]
                sums[j + b][a][c] = x if old is None else old + x
        new = {}
        for j in range(first + 1, final):
            s = sums[j]
            row = [s[0][c] + mv.below(s[1][c]) for c in range(2)]
            row[0] = row[0] + mv.before(row[1])
            new[j] = [value[j][g] + inverse[j][g] * (load[j][g] - row[g]) for g in range(2)]
        value = new
    for j in value:
        value[j][1] = mv.after(value[j][0], value[j][1])
    lines = [[mv.pick(value[5 + m][g], value[6 + m][g]) for g in range(2)] for m in range(4)]
    return lines, mv.pick(coeffs[5], coeffs[6]), mv.pick(coeffs[7], coeffs[8])


def butterfly(v, axis):
    out = {}
    for key in v:
        if key[axis]:
            continue
        up = tuple(1 if k == axis else key[k] for k in range(3))
        x, y = v[key], v[up]
        out[key] = y if x is None else x + y
        out[up] = -y if x is None else x - y
    return out


def nodal(mv, pair, count):
    rows = []
    up = [mv.above(v) for v in pair]
    for a in range(count):
        lo, hi = float(INTERP[a, 0]), float(INTERP[a, 1])
        if a == 0:
            ends = pair
        elif a == 4:
            ends = up
        else:
            ends = [lo * pair[g] + hi * up[g] for g in range(2)]
        rows.append([ends[0] if c == 0 else ends[1] if c == 4 else float(INTERP[c, 0]) * ends[0] + float(INTERP[c, 1]) * ends[1] for c in range(N)])
    return rows


def neighbour_face(mv, near, far, coeff):
    w = [float(x) for x in weights]
    x = nodal(mv, near, N)
    z = nodal(mv, far, N)
    y = []
    for a in range(N):
        row = []
        for c in range(N):
            v = (x[a][c] - z[a][c]) * (0.5 * weight(a, c))
            if a in (0, 4):
                v = v + (x[a][c] - x[4 - a][c]) * (0.5 * w[0] * w[SYM[c]])
            if c in (0, 4):
                v = v + (x[a][c] - x[a][4 - c]) * (0.5 * w[0] * w[SYM[a]])
            row.append(v * coeff)
        y.append(row)
    out = []
    for a in range(4):
        row = [y[0][c] + mv.below(y[4][c]) for c in range(N)] if a == 0 else y[a]
        row[0] = row[0] + mv.before(row[4])
        out.extend(row)
    return out


def correct_kernel(strips, info, u_ref, f_ref, inv_ref, coeff_ref, ga_ref, near_ref, chip_ref, mine_ref, other_ref, un_ref, yn_ref, a_ref, b_ref, ua_ref, ya_ref, face_ref, acc_ref, up_ref):
    mv = Moves(info)
    coeff = coeff_ref[...]
    lines, coeff_left, coeff_right = coarse_solve(mv, strips, chip_ref, mine_ref, other_ref)
    for k, v in enumerate(neighbour_face(mv, lines[1], lines[0], coeff_left)):
        face_ref[k] = v
    for k, v in enumerate(neighbour_face(mv, lines[2], lines[3], coeff_right)):
        face_ref[20 + k] = v
    low, high = nodal(mv, lines[1], 4), nodal(mv, lines[2], 4)
    for a in range(4):
        for b in range(N):
            for c in range(N):
                if b == 0:
                    v = low[a][c]
                elif b == 4:
                    v = high[a][c]
                else:
                    v = float(INTERP[b, 0]) * low[a][c] + float(INTERP[b, 1]) * high[a][c]
                ua_ref[at(a, b, c)] = u_ref[at(a, b, c)] + v
    apply_operator(mv, ua_ref, coeff, ya_ref, acc_ref, up_ref)
    left, right = got_faces(mv, ga_ref, near_ref, 20, strips, 5, 10)
    left = [left[k] + face_ref[k] for k in range(20)]
    right = [right[k] + face_ref[20 + k] for k in range(20)]
    smooth(mv, ua_ref, f_ref, ya_ref, left, right, inv_ref, un_ref)
    apply_operator(mv, un_ref, coeff, yn_ref, acc_ref, up_ref)
    put_faces(mv, yn_ref, a_ref, b_ref)


def residual_kernel(strips, info, y_ref, f_ref, ga_ref, gb_ref, half_ref, r_ref):
    mv = Moves(info)
    left, right = got_faces(mv, ga_ref, gb_ref, 20, strips)
    for a in range(4):
        for b in range(N):
            r = residual_row(mv, f_ref, y_ref, left, right, a, b)
            r[4] = mv.after(r[0], r[4])
            for c in range(N):
                r_ref[at(a, b, c)] = r[c]
    half_rows(mv, r_ref, half_ref)


def spread_kernel(half_ref, out_ref):
    out_ref[pl.ds(0, 400)] = half_ref[...]
    row = lax.broadcasted_iota(jnp.int32, (100, 128), 0)
    out_ref[pl.ds(400, 100)] = jnp.where((row & 3) == 3, 0.0, half_ref[pl.ds(1, 100)])


VM = pl.BlockSpec(memory_space=pltpu.VMEM)
SM = pl.BlockSpec(memory_space=pltpu.SMEM)
FIELD = (100, 8, 128)
WORK = [(125, 8, 128), (25, 8, 128)]


def call(name, kernel, outs, scratch, info, *args):
    specs = [VM] * len(args)
    operands = args
    if info is not None:
        specs, operands = [SM] + specs, (info, *args)
    return pl.pallas_call(
        kernel,
        out_shape=[jax.ShapeDtypeStruct(s, F32) for s in outs],
        in_specs=specs,
        out_specs=[VM] * len(outs),
        scratch_shapes=[pltpu.VMEM(s, F32) for s in scratch],
        compiler_params=pltpu.CompilerParams(vmem_limit_bytes=12 * 1024 * 1024),
        name=name,
    )(*operands)


def placement(sizes):
    _, ey, lin = sizes
    if (ey, lin) != (2, 64):
        return list(range(ey * lin))
    order = []
    for q in range(64):
        side, p, y = q // 32, (q % 32) // 4, q % 4
        z = p if side == 0 else 7 - p
        order.append(side * 64 + z * 8 + (y if p % 2 == 0 else 3 - y) * 2)
    return [order[s // 2] + s % 2 for s in range(128)]


def per_device(sizes):
    strips = sizes[1] * sizes[2]
    chips = strips // 2
    place = placement(sizes)
    device = [[copy * strips + place[s] for s in range(strips)] for copy in range(2)]
    to_same = [(e * strips + s, device[e][s]) for e in range(2) for s in range(strips)]
    to_other = [(e * strips + s, device[1 - e][s]) for e in range(2) for s in range(strips)]
    back = [(b, a) for a, b in to_same]
    within = [(device[e][s], device[e][s ^ 1]) for e in range(2) for s in range(strips)]

    def chip_pairs(d):
        pairs = []
        for e in range(2):
            for s in range(strips):
                k = (s // 2 - d) % chips if s % 2 == 0 else (s // 2 + d) % chips
                pairs.append((device[e][s], device[e][2 * k + 1 - s % 2]))
        return pairs

    beyond = {d: chip_pairs(d) for d in (1, 2, 3)}
    table = np.zeros((2 * strips, 4), np.int32)
    for copy in range(2):
        for s in range(strips):
            table[device[copy][s], :3] = (s % 2, copy, s)

    def swap(x, pairs):
        return lax.ppermute(x, AXES, pairs)

    def run(load, kappa, wet):
        info = lax.dynamic_index_in_dim(jnp.asarray(table), lax.axis_index(AXES), 0, keepdims=False)
        (packed,) = call("pack", pack_kernel, [(408, 128)], [], None, load.reshape(500, 128), kappa.reshape(4, 128), wet.reshape(4, 128))
        same, other = swap(packed, to_same), swap(packed, to_other)
        part, coeff, a, b = call("unpack", unpack_kernel, [FIELD, (8, 128), (21, 8, 128), (21, 8, 128)], [], info, same, other)
        faces = [(20, 8, 128), (20, 8, 128)]

        def bound(kernel):
            def body(*refs):
                kernel(strips, *refs)
            return body

        def trade(a, b):
            return swap(a, within), swap(b, beyond[1])

        a, b = trade(a, b)
        u, y, f, inv, a, b = call("first", bound(first_kernel), [FIELD, FIELD, FIELD, (12, 8, 128), *faces], WORK, info, part, coeff, a, b)

        def sweep(u, y, a, b):
            a, b = trade(a, b)
            return call("sweep", bound(sweep_kernel), [FIELD, FIELD, *faces], WORK, info, u, y, f, inv, coeff, a, b)

        def sweep_and_correct(u, y, a, b):
            a, b = trade(a, b)
            u, own, a, b = call("restrict", bound(restrict_kernel), [FIELD, (5, 8, 128), (25, 8, 128), (25, 8, 128)], [FIELD, *WORK], info, u, y, f, inv, coeff, a, b, part)
            a = swap(a, within)
            chip, near = call("chip", chip_kernel, [(10, 8, 128), (30, 8, 128)], [], info, own, a, b)
            near, second, third = swap(near, beyond[1]), swap(chip, beyond[2]), swap(chip, beyond[3])
            (mine,) = call("side", side_kernel, [(30, 8, 128)], [], None, near, second, third)
            theirs = swap(mine, within)
            return call("correct", bound(correct_kernel), [FIELD, FIELD, *faces], [FIELD, FIELD, (40, 8, 128), *WORK], info, u, f, inv, coeff, a, near, chip, mine, theirs)

        u, y, a, b = sweep_and_correct(u, y, a, b)
        u, y, a, b = sweep(u, y, a, b)
        u, y, a, b = sweep(u, y, a, b)
        u, y, a, b = sweep_and_correct(u, y, a, b)
        a, b = trade(a, b)
        y, a, b, half = call("last", bound(last_sweep_kernel), [FIELD, *faces, (400, 128)], [FIELD, *WORK], info, u, y, f, inv, coeff, a, b)
        a, b = trade(a, b)
        half = swap(half, back)
        (left_half,) = call("residual", bound(residual_kernel), [(400, 128)], [FIELD], info, y, f, a, b)
        (solved,) = call("spread", spread_kernel, [(500, 128)], [], None, half)
        (rest,) = call("spread", spread_kernel, [(500, 128)], [], None, swap(left_half, back))
        return solved.reshape(load.shape), rest.reshape(load.shape)

    return run


def solution(mesh):
    sizes = tuple(mesh.shape[name] for name in AXES)
    whole = P(None, None, None, None, ("ey", "lin"), "ex")
    flat = P(None, ("ey", "lin"), "ex")
    return jax.shard_map(per_device(sizes), mesh=mesh, in_specs=(whole, flat, flat), out_specs=(whole, whole), check_vma=False)
```

```python
import math

import jax
import jax.numpy as jnp
import numpy as np
from jax import lax
from jax.experimental import pallas as pl
from jax.experimental.pallas import tpu as pltpu
from jax.sharding import PartitionSpec as P

AXES = ("ex", "ey", "lin")
N = 5
NC = 4
WIN = 14
FINE_RELAX = 0.25
COARSE_RELAX = 0.4
F32 = jnp.float32

points = np.array([-1.0, -math.sqrt(3.0 / 7.0), 0.0, math.sqrt(3.0 / 7.0), 1.0])
weights = np.array([0.1, 49.0 / 90.0, 32.0 / 45.0, 49.0 / 90.0, 0.1])


def stiffness():
    eye = np.eye(N)
    spread = points[:, None] - points[None, :] + eye
    factors = np.prod(spread, axis=1)
    deriv = factors[:, None] / (factors[None, :] * spread)
    deriv = np.where(eye > 0, (np.sum(1.0 / spread, axis=1) - 1.0)[:, None], deriv)
    return deriv.T @ (weights[:, None] * deriv)


STIFF = stiffness()
LINE = STIFF / weights[:, None]
EVEN = [[float(LINE[i, j] + LINE[i, 4 - j]) / 2 for j in range(2)] for i in range(3)]
ODD = [[float(LINE[i, j] - LINE[i, 4 - j]) / 2 for j in range(2)] for i in range(2)]
INTERP = np.stack([(1.0 - points) / 2.0, (1.0 + points) / 2.0], axis=1)
SYM = [0, 1, 2, 1, 0]


def weight(*nodes):
    return float(np.prod([weights[SYM[k]] for k in sorted(SYM[n] for n in nodes)]))


def inverse_factor(a, b, c):
    s, w = np.diag(STIFF), weights
    a, b, c = sorted(SYM[n] for n in (a, b, c))
    return FINE_RELAX / float(s[a] * w[b] * w[c] + w[a] * s[b] * w[c] + w[a] * w[b] * s[c])


def at(a, b, c):
    return a * 25 + b * 5 + c


def line(u):
    m2 = u[2] + u[2]
    e0, e1 = u[0] + u[4] - m2, u[1] + u[3] - m2
    o0, o1 = u[0] - u[4], u[1] - u[3]
    even = [EVEN[i][0] * e0 + EVEN[i][1] * e1 for i in range(3)]
    odd = [ODD[i][0] * o0 + ODD[i][1] * o1 for i in range(2)]
    return [even[0] + odd[0], even[1] + odd[1], even[2], even[1] - odd[1], even[0] - odd[0]]


class Moves:
    def __init__(self, marks=None):
        sub = lax.broadcasted_iota(jnp.int32, (8, 128), 0)
        lane = lax.broadcasted_iota(jnp.int32, (8, 128), 1)
        self.low = sub < 4
        self.top = (sub & 3) == 3
        self.bottom = (sub & 3) == 0
        self.lane_first = lane == 0
        self.lane_last = lane == 127
        self.last = jnp.logical_and(lane == 127, sub >= 4)
        self.marks = marks
        if marks is not None:
            self.even = marks[0] > 0.5
            self.copy0 = marks[1] > 0.5

    def above(self, x):
        return jnp.where(self.top, 0.0, pltpu.roll(x, 7, 0))

    def below(self, x):
        return jnp.where(self.bottom, 0.0, pltpu.roll(x, 1, 0))

    def before(self, x):
        r = pltpu.roll(x, 1, 1)
        return jnp.where(self.lane_first, jnp.where(self.low, 0.0, pltpu.roll(r, 4, 0)), r)

    def after(self, x, end):
        r = pltpu.roll(x, 127, 1)
        return jnp.where(self.lane_last, jnp.where(self.low, pltpu.roll(r, 4, 0), end), r)

    def pick(self, x, y):
        return jnp.where(self.even, x, y)


def apply_operator(mv, u_ref, coeff, y_ref, acc_ref, up_ref):
    for b in range(N):
        for c in range(N):
            u = [u_ref[at(a, b, c)] for a in range(4)]
            u.append(mv.above(u[0]))
            up_ref[b * 5 + c] = u[4]
            for a, value in enumerate(line(u)):
                acc_ref[at(a, b, c)] = value
    for a in (4, 0, 1, 2, 3):
        scale = {}
        for b in range(3):
            for c in range(b, 3):
                scale[b, c] = scale[c, b] = coeff * weight(a, b, c)
        u = [[up_ref[b * 5 + c] if a == 4 else u_ref[at(a, b, c)] for c in range(N)] for b in range(N)]
        across = [line([u[b][c] for b in range(N)]) for c in range(N)]
        for b in range(N):
            along = line(u[b])
            y = [(acc_ref[at(a, b, c)] + along[c] + across[c][b]) * scale[SYM[b], SYM[c]] for c in range(N)]
            if a == 4:
                for c in range(N):
                    up_ref[b * 5 + c] = y[c]
                continue
            if a == 0:
                y = [y[c] + mv.below(up_ref[b * 5 + c]) for c in range(N)]
            y[0] = y[0] + mv.before(y[4])
            for c in range(N):
                y_ref[at(a, b, c)] = y[c]


def put_faces(mv, y_ref, a_ref, b_ref, first=0):
    for a in range(4):
        for c in range(N):
            low, high = y_ref[at(a, 0, c)], y_ref[at(a, 4, c)]
            a_ref[first + a * 5 + c] = mv.pick(high, low)
            b_ref[first + a * 5 + c] = mv.pick(low, high)


def got_faces(mv, a_ref, b_ref, count, a_first=0, b_first=0):
    has_left, has_right = mv.marks[2], mv.marks[3]
    left, right = [], []
    for k in range(count):
        x, y = a_ref[a_first + k], b_ref[b_first + k]
        left.append(mv.pick(y, x) * has_left)
        right.append(mv.pick(x, y) * has_right)
    return left, right


def inverse_at(inv_ref, a, b, c):
    kind = (0 if a == 0 else 6) + (0 if b == 0 else 4 if b == 4 else 2) + (0 if c == 0 else 1)
    return inv_ref[kind] * inverse_factor(a, b, c)


def residual_row(mv, f_ref, y_ref, left, right, a, b):
    row = []
    for c in range(N):
        r = f_ref[at(a, b, c)] - y_ref[at(a, b, c)]
        if b == 0:
            r = r - left[a * 5 + c]
        if b == 4:
            r = r - right[a * 5 + c]
        row.append(r)
    return row


def smooth(mv, u_ref, f_ref, y_ref, left, right, inv_ref, out_ref):
    for a in range(4):
        for b in range(N):
            r = residual_row(mv, f_ref, y_ref, left, right, a, b)
            u = [u_ref[at(a, b, c)] + r[c] * inverse_at(inv_ref, a, b, c) for c in range(N)]
            u[4] = mv.after(u[0], u[4])
            for c in range(N):
                out_ref[at(a, b, c)] = u[c]


def half_rows(mv, ref, out_ref):
    for n in range(0, 100, 2):
        x, y = ref[n], ref[n + 1]
        x = jnp.where(mv.copy0, x, pltpu.roll(x, 4, 0))
        y = jnp.where(mv.copy0, pltpu.roll(y, 4, 0), y)
        out_ref[pl.ds(4 * n, 8)] = jnp.where(mv.low, x, y)


def pack_kernel(load_ref, out_ref):
    row = lax.broadcasted_iota(jnp.int32, (100, 128), 0)
    out_ref[pl.ds(0, 100)] = load_ref[pl.ds(0, 100)] + jnp.where((row & 3) == 0, 0.0, load_ref[pl.ds(399, 100)])
    out_ref[pl.ds(100, 300)] = load_ref[pl.ds(100, 300)]
    coeff = load_ref[pl.ds(500, 4)]
    out_ref[pl.ds(400, 4)] = coeff
    out_ref[pl.ds(404, 4)] = coeff


def unpack_kernel(marks, same_ref, other_ref, f_ref, coeff_ref, a_ref, b_ref):
    mv = Moves(marks)

    def pair(n):
        x, y = same_ref[pl.ds(4 * n, 8)], other_ref[pl.ds(4 * n, 8)]
        h0, h1 = jnp.where(mv.copy0, x, y), jnp.where(mv.copy0, y, x)
        return jnp.where(mv.low, h0, pltpu.roll(h1, 4, 0)), jnp.where(mv.low, pltpu.roll(h0, 4, 0), h1)

    for n in range(0, 100, 2):
        f_ref[n], f_ref[n + 1] = pair(n)
    coeff, _ = pair(100)
    coeff_ref[...] = coeff
    for a in range(4):
        for b in range(N):
            f_ref[at(a, b, 0)] = f_ref[at(a, b, 0)] + mv.before(f_ref[at(a, b, 4)])
    put_faces(mv, f_ref, a_ref, b_ref)
    a_ref[20] = coeff
    b_ref[20] = coeff


def first_kernel(marks, part_ref, coeff_ref, ga_ref, gb_ref, u_ref, y_ref, f_ref, inv_ref, a_ref, b_ref, acc_ref, up_ref):
    mv = Moves(marks)
    left, right = got_faces(mv, ga_ref, gb_ref, 21)
    coeff = coeff_ref[...]
    for kind_b, value in enumerate((coeff + left[20], coeff, coeff + right[20])):
        for kind_a, v in enumerate((value + mv.below(value), value)):
            inv_ref[kind_a * 6 + kind_b * 2] = 1.0 / (v + mv.before(v))
            inv_ref[kind_a * 6 + kind_b * 2 + 1] = 1.0 / v
    for a in range(4):
        for b in range(N):
            f = [part_ref[at(a, b, c)] for c in range(N)]
            if b == 0:
                f = [f[c] + left[a * 5 + c] for c in range(N)]
            if b == 4:
                f = [f[c] + right[a * 5 + c] for c in range(N)]
            u = [f[c] * inverse_at(inv_ref, a, b, c) for c in range(N)]
            u[4] = mv.after(u[0], u[4])
            for c in range(N):
                f_ref[at(a, b, c)] = f[c]
                u_ref[at(a, b, c)] = u[c]
    apply_operator(mv, u_ref, coeff, y_ref, acc_ref, up_ref)
    put_faces(mv, y_ref, a_ref, b_ref)


def sweep_kernel(marks, u_ref, y_ref, f_ref, inv_ref, coeff_ref, ga_ref, gb_ref, un_ref, yn_ref, a_ref, b_ref, acc_ref, up_ref):
    mv = Moves(marks)
    left, right = got_faces(mv, ga_ref, gb_ref, 20)
    smooth(mv, u_ref, f_ref, y_ref, left, right, inv_ref, un_ref)
    apply_operator(mv, un_ref, coeff_ref[...], yn_ref, acc_ref, up_ref)
    put_faces(mv, yn_ref, a_ref, b_ref)


def last_sweep_kernel(marks, u_ref, y_ref, f_ref, inv_ref, coeff_ref, ga_ref, gb_ref, yn_ref, a_ref, b_ref, half_ref, un_ref, acc_ref, up_ref):
    sweep_kernel(marks, u_ref, y_ref, f_ref, inv_ref, coeff_ref, ga_ref, gb_ref, un_ref, yn_ref, a_ref, b_ref, acc_ref, up_ref)
    half_rows(Moves(marks), un_ref, half_ref)


def restrict_kernel(marks, u_ref, y_ref, f_ref, inv_ref, coeff_ref, ga_ref, gb_ref, part_ref, un_ref, own_ref, a_ref, b_ref, yn_ref, acc_ref, up_ref):
    mv = Moves(marks)
    left, right = got_faces(mv, ga_ref, gb_ref, 20)
    smooth(mv, u_ref, f_ref, y_ref, left, right, inv_ref, un_ref)
    apply_operator(mv, un_ref, coeff_ref[...], yn_ref, acc_ref, up_ref)
    put_faces(mv, yn_ref, a_ref, b_ref, 5)
    z = [[], []]
    for c in range(N):
        rows = [[], []]
        for a in range(4):
            r = [part_ref[at(a, b, c)] - yn_ref[at(a, b, c)] for b in range(N)]
            inner = [sum(float(INTERP[b, side]) * r[b] for b in (1, 2, 3)) for side in range(2)]
            rows[0].append(r[0] + inner[0])
            rows[1].append(r[4] + inner[1])
        for side in range(2):
            x = rows[side]
            low = x[0] + sum(float(INTERP[a, 0]) * x[a] for a in (1, 2, 3))
            z[side].append(low + mv.below(sum(float(INTERP[a, 1]) * x[a] for a in (1, 2, 3))))
    for side in range(2):
        x = z[side]
        inner = [sum(float(INTERP[c, k]) * x[c] for c in (1, 2, 3)) for k in range(2)]
        own_ref[side * 2] = x[0] + inner[0] + mv.before(inner[1])
        own_ref[side * 2 + 1] = jnp.where(mv.last, x[4] + inner[1], 0.0)
    own_ref[4] = coeff_ref[...]
    for k in range(5):
        a_ref[k] = own_ref[k]


def chip_kernel(marks, own_ref, ga_ref, b_ref, chip_ref, near_ref):
    mv = Moves(marks)
    for k in range(5):
        x, y = own_ref[k], ga_ref[k]
        low, high = mv.pick(x, y), mv.pick(y, x)
        chip_ref[k] = low
        chip_ref[5 + k] = high
        near_ref[k] = low
        near_ref[5 + k] = high
    for k in range(20):
        near_ref[10 + k] = b_ref[5 + k]


def side_kernel(near_ref, second_ref, third_ref, out_ref):
    for k in range(10):
        out_ref[k] = near_ref[k]
        out_ref[10 + k] = second_ref[k]
        out_ref[20 + k] = third_ref[k]


def coarse_solve(mv, chip_ref, mine_ref, other_ref):
    window = []
    for w in range(WIN):
        rows = []
        ok = mv.marks[4 + w]
        for k in range(5):
            if w in (6, 7):
                rows.append(chip_ref[(w - 6) * 5 + k])
                continue
            if w < 6:
                slot = (2 - w // 2) * 10 + (w % 2) * 5 + k
                x = mv.pick(mine_ref[slot], other_ref[slot])
            else:
                slot = (w // 2 - 4) * 10 + (w % 2) * 5 + k
                x = mv.pick(other_ref[slot], mine_ref[slot])
            rows.append(x * ok)
        window.append(rows)
    coeffs = [rows[4] for rows in window]
    load, inverse, value = {}, {}, {}
    factor = COARSE_RELAX / (2.0 / 3.0)
    for j in range(2, 13):
        load[j] = [window[j - 1][2 + g] + window[j][g] for g in range(2)]
        k = coeffs[j - 1] + coeffs[j]
        k = k + mv.below(k)
        inverse[j] = [jnp.where(v > 0.0, factor / v, 0.0) for v in (k + mv.before(k), k)]
        value[j] = [inverse[j][g] * load[j][g] for g in range(2)]
    for step in range(NC - 1):
        first, final = 2 + step, 12 - step
        nodes = {}
        for j in range(first, final + 1):
            value[j][1] = mv.after(value[j][0], value[j][1])
            nodes[j] = [value[j], [mv.above(v) for v in value[j]]]
        sums = {j: [[None, None], [None, None]] for j in range(first, final + 1)}
        for j in range(first, final):
            v = {(a, b, c): nodes[j + b][a][c] for a in range(2) for b in range(2) for c in range(2)}
            for axis in range(3):
                v = butterfly(v, axis)
            cf = [coeffs[j] * 0.125, coeffs[j] * (0.125 * 2.0 / 3.0), coeffs[j] * (0.125 / 3.0)]
            v = {key: None if sum(key) == 0 else x * cf[sum(key) - 1] for key, x in v.items()}
            for axis in range(3):
                v = butterfly(v, axis)
            for (a, b, c), x in v.items():
                old = sums[j + b][a][c]
                sums[j + b][a][c] = x if old is None else old + x
        new = {}
        for j in range(first + 1, final):
            s = sums[j]
            row = [s[0][c] + mv.below(s[1][c]) for c in range(2)]
            row[0] = row[0] + mv.before(row[1])
            new[j] = [value[j][g] + inverse[j][g] * (load[j][g] - row[g]) for g in range(2)]
        value = new
    for j in value:
        value[j][1] = mv.after(value[j][0], value[j][1])
    lines = [[mv.pick(value[5 + m][g], value[6 + m][g]) for g in range(2)] for m in range(4)]
    return lines, mv.pick(coeffs[5], coeffs[6]), mv.pick(coeffs[7], coeffs[8])


def butterfly(v, axis):
    out = {}
    for key in v:
        if key[axis]:
            continue
        up = tuple(1 if k == axis else key[k] for k in range(3))
        x, y = v[key], v[up]
        out[key] = y if x is None else x + y
        out[up] = -y if x is None else x - y
    return out


def nodal(mv, pair, count):
    rows = []
    up = [mv.above(v) for v in pair]
    for a in range(count):
        lo, hi = float(INTERP[a, 0]), float(INTERP[a, 1])
        if a == 0:
            ends = pair
        elif a == 4:
            ends = up
        else:
            ends = [lo * pair[g] + hi * up[g] for g in range(2)]
        rows.append([ends[0] if c == 0 else ends[1] if c == 4 else float(INTERP[c, 0]) * ends[0] + float(INTERP[c, 1]) * ends[1] for c in range(N)])
    return rows


def neighbour_face(mv, near, far, coeff):
    w = [float(x) for x in weights]
    x = nodal(mv, near, N)
    z = nodal(mv, far, N)
    y = []
    for a in range(N):
        row = []
        for c in range(N):
            v = (x[a][c] - z[a][c]) * (0.5 * weight(a, c))
            if a in (0, 4):
                v = v + (x[a][c] - x[4 - a][c]) * (0.5 * w[0] * w[SYM[c]])
            if c in (0, 4):
                v = v + (x[a][c] - x[a][4 - c]) * (0.5 * w[0] * w[SYM[a]])
            row.append(v * coeff)
        y.append(row)
    out = []
    for a in range(4):
        row = [y[0][c] + mv.below(y[4][c]) for c in range(N)] if a == 0 else y[a]
        row[0] = row[0] + mv.before(row[4])
        out.extend(row)
    return out


def correct_kernel(marks, u_ref, f_ref, inv_ref, coeff_ref, ga_ref, near_ref, chip_ref, mine_ref, other_ref, un_ref, yn_ref, a_ref, b_ref, ua_ref, ya_ref, face_ref, acc_ref, up_ref):
    mv = Moves(marks)
    coeff = coeff_ref[...]
    lines, coeff_left, coeff_right = coarse_solve(mv, chip_ref, mine_ref, other_ref)
    for k, v in enumerate(neighbour_face(mv, lines[1], lines[0], coeff_left)):
        face_ref[k] = v
    for k, v in enumerate(neighbour_face(mv, lines[2], lines[3], coeff_right)):
        face_ref[20 + k] = v
    low, high = nodal(mv, lines[1], 4), nodal(mv, lines[2], 4)
    for a in range(4):
        for b in range(N):
            for c in range(N):
                if b == 0:
                    v = low[a][c]
                elif b == 4:
                    v = high[a][c]
                else:
                    v = float(INTERP[b, 0]) * low[a][c] + float(INTERP[b, 1]) * high[a][c]
                ua_ref[at(a, b, c)] = u_ref[at(a, b, c)] + v
    apply_operator(mv, ua_ref, coeff, ya_ref, acc_ref, up_ref)
    left, right = got_faces(mv, ga_ref, near_ref, 20, 5, 10)
    left = [left[k] + face_ref[k] for k in range(20)]
    right = [right[k] + face_ref[20 + k] for k in range(20)]
    smooth(mv, ua_ref, f_ref, ya_ref, left, right, inv_ref, un_ref)
    apply_operator(mv, un_ref, coeff, yn_ref, acc_ref, up_ref)
    put_faces(mv, yn_ref, a_ref, b_ref)


def residual_kernel(marks, y_ref, f_ref, ga_ref, gb_ref, half_ref, r_ref):
    mv = Moves(marks)
    left, right = got_faces(mv, ga_ref, gb_ref, 20)
    for a in range(4):
        for b in range(N):
            r = residual_row(mv, f_ref, y_ref, left, right, a, b)
            r[4] = mv.after(r[0], r[4])
            for c in range(N):
                r_ref[at(a, b, c)] = r[c]
    half_rows(mv, r_ref, half_ref)


def spread_kernel(half_ref, out_ref):
    out_ref[pl.ds(0, 400)] = half_ref[...]
    row = lax.broadcasted_iota(jnp.int32, (100, 128), 0)
    out_ref[pl.ds(400, 100)] = jnp.where((row & 3) == 3, 0.0, half_ref[pl.ds(1, 100)])


VM = pl.BlockSpec(memory_space=pltpu.VMEM)
FIELD = (100, 8, 128)
WORK = [(125, 8, 128), (25, 8, 128)]


def call(name, kernel, outs, scratch, *args):
    return pl.pallas_call(
        kernel,
        out_shape=[jax.ShapeDtypeStruct(s, F32) for s in outs],
        in_specs=[VM] * len(args),
        out_specs=[VM] * len(outs),
        scratch_shapes=[pltpu.VMEM(s, F32) for s in scratch],
        compiler_params=pltpu.CompilerParams(vmem_limit_bytes=12 * 1024 * 1024),
        name=name,
    )(*args)


MODE = "flip"


def placement(sizes):
    _, ey, lin = sizes
    place = list(range(ey * lin))
    if lin == 64 and MODE == "flip":
        for s in range(ey * lin):
            z, y, core = s // 8 % 8, s // 2 % 4, s % 2
            if z % 2:
                place[s] = s - y * 2 + (3 - y) * 2
    return place


def per_device(sizes):
    strips = sizes[1] * sizes[2]
    chips = strips // 2
    place = placement(sizes)
    device = [[copy * strips + place[s] for s in range(strips)] for copy in range(2)]
    to_same = [(e * strips + s, device[e][s]) for e in range(2) for s in range(strips)]
    to_other = [(e * strips + s, device[1 - e][s]) for e in range(2) for s in range(strips)]
    back = [(b, a) for a, b in to_same]
    within = [(device[e][s], device[e][s ^ 1]) for e in range(2) for s in range(strips)]

    def chip_pairs(d):
        pairs = []
        for e in range(2):
            for s in range(strips):
                k = s // 2 - d if s % 2 == 0 else s // 2 + d
                if 0 <= k < chips:
                    pairs.append((device[e][s], device[e][2 * k + 1 - s % 2]))
                else:
                    pairs.append((device[e][s], device[1 - e][s]))
        return pairs

    beyond = {d: chip_pairs(d) for d in (1, 2, 3)}
    table = np.zeros((2 * strips, 4 + WIN), np.float32)
    for copy in range(2):
        for s in range(strips):
            window = [0 <= s - s % 2 - 6 + w < strips for w in range(WIN)]
            table[device[copy][s]] = [s % 2 == 0, copy == 0, s > 0, s < strips - 1, *window]

    def swap(x, pairs):
        return lax.ppermute(x, AXES, pairs)

    def restore(x):
        return x if place == sorted(place) else swap(x, back)

    def run(load, kappa, wet):
        marks = lax.dynamic_index_in_dim(jnp.asarray(table), lax.axis_index(AXES), 0, keepdims=False)
        marks = jnp.broadcast_to(marks[:, None, None], (4 + WIN, 8, 128))
        coeff = kappa * jnp.where(wet == 1, 1.0, 0.05).astype(F32)
        packed = jnp.concatenate([load.reshape(500, 1, 128), coeff.reshape(4, 1, 128)]).reshape(504, 128)
        (packed,) = call("pack", pack_kernel, [(408, 128)], [], packed)
        same, other = packed if place == sorted(place) else swap(packed, to_same), swap(packed, to_other)
        part, coeff, a, b = call("unpack", unpack_kernel, [FIELD, (8, 128), (21, 8, 128), (21, 8, 128)], [], marks, same, other)
        faces = [(20, 8, 128), (20, 8, 128)]

        def trade(a, b):
            return swap(a, within), swap(b, beyond[1])

        a, b = trade(a, b)
        u, y, f, inv, a, b = call("first", first_kernel, [FIELD, FIELD, FIELD, (12, 8, 128), *faces], WORK, marks, part, coeff, a, b)

        def sweep(u, y, a, b):
            a, b = trade(a, b)
            return call("sweep", sweep_kernel, [FIELD, FIELD, *faces], WORK, marks, u, y, f, inv, coeff, a, b)

        def sweep_and_correct(u, y, a, b):
            a, b = trade(a, b)
            u, own, a, b = call("restrict", restrict_kernel, [FIELD, (5, 8, 128), (25, 8, 128), (25, 8, 128)], [FIELD, *WORK], marks, u, y, f, inv, coeff, a, b, part)
            a = swap(a, within)
            chip, near = call("chip", chip_kernel, [(10, 8, 128), (30, 8, 128)], [], marks, own, a, b)
            near, second, third = swap(near, beyond[1]), swap(chip, beyond[2]), swap(chip, beyond[3])
            (mine,) = call("side", side_kernel, [(30, 8, 128)], [], near, second, third)
            theirs = swap(mine, within)
            return call("correct", correct_kernel, [FIELD, FIELD, *faces], [FIELD, FIELD, (40, 8, 128), *WORK], marks, u, f, inv, coeff, a, near, chip, mine, theirs)

        u, y, a, b = sweep_and_correct(u, y, a, b)
        u, y, a, b = sweep(u, y, a, b)
        u, y, a, b = sweep(u, y, a, b)
        u, y, a, b = sweep_and_correct(u, y, a, b)
        a, b = trade(a, b)
        y, a, b, half = call("last", last_sweep_kernel, [FIELD, *faces, (400, 128)], [FIELD, *WORK], marks, u, y, f, inv, coeff, a, b)
        a, b = trade(a, b)
        half = restore(half)
        (left_half,) = call("residual", residual_kernel, [(400, 128)], [FIELD], marks, y, f, a, b)
        (solved,) = call("spread", spread_kernel, [(500, 128)], [], half)
        (rest,) = call("spread", spread_kernel, [(500, 128)], [], restore(left_half))
        return solved.reshape(load.shape), rest.reshape(load.shape)

    return run


def solution(mesh):
    sizes = tuple(mesh.shape[name] for name in AXES)
    whole = P(None, None, None, None, ("ey", "lin"), "ex")
    flat = P(None, ("ey", "lin"), "ex")
    return jax.shard_map(per_device(sizes), mesh=mesh, in_specs=(whole, flat, flat), out_specs=(whole, whole), check_vma=False)
```

```python
import math

import jax
import jax.numpy as jnp
import numpy as np
from jax import lax
from jax.experimental import pallas as pl
from jax.experimental.pallas import tpu as pltpu
from jax.sharding import PartitionSpec as P

AXES = ("ex", "ey", "lin")
N = 5
NC = 4
WIN = 14
FINE_RELAX = 0.25
COARSE_RELAX = 0.4
F32 = jnp.float32

points = np.array([-1.0, -math.sqrt(3.0 / 7.0), 0.0, math.sqrt(3.0 / 7.0), 1.0])
weights = np.array([0.1, 49.0 / 90.0, 32.0 / 45.0, 49.0 / 90.0, 0.1])


def stiffness():
    eye = np.eye(N)
    spread = points[:, None] - points[None, :] + eye
    factors = np.prod(spread, axis=1)
    deriv = factors[:, None] / (factors[None, :] * spread)
    deriv = np.where(eye > 0, (np.sum(1.0 / spread, axis=1) - 1.0)[:, None], deriv)
    return deriv.T @ (weights[:, None] * deriv)


STIFF = stiffness()
LINE = STIFF / weights[:, None]
EVEN = [[float(LINE[i, j] + LINE[i, 4 - j]) / 2 for j in range(2)] for i in range(3)]
ODD = [[float(LINE[i, j] - LINE[i, 4 - j]) / 2 for j in range(2)] for i in range(2)]
INTERP = np.stack([(1.0 - points) / 2.0, (1.0 + points) / 2.0], axis=1)
SYM = [0, 1, 2, 1, 0]


def weight(*nodes):
    return float(np.prod([weights[SYM[k]] for k in sorted(SYM[n] for n in nodes)]))


def inverse_factor(a, b, c):
    s, w = np.diag(STIFF), weights
    a, b, c = sorted(SYM[n] for n in (a, b, c))
    return FINE_RELAX / float(s[a] * w[b] * w[c] + w[a] * s[b] * w[c] + w[a] * w[b] * s[c])


def at(a, b, c):
    return a * 25 + b * 5 + c


def line(u):
    m2 = u[2] + u[2]
    e0, e1 = u[0] + u[4] - m2, u[1] + u[3] - m2
    o0, o1 = u[0] - u[4], u[1] - u[3]
    even = [EVEN[i][0] * e0 + EVEN[i][1] * e1 for i in range(3)]
    odd = [ODD[i][0] * o0 + ODD[i][1] * o1 for i in range(2)]
    return [even[0] + odd[0], even[1] + odd[1], even[2], even[1] - odd[1], even[0] - odd[0]]


class Moves:
    def __init__(self, marks=None):
        sub = lax.broadcasted_iota(jnp.int32, (8, 128), 0)
        lane = lax.broadcasted_iota(jnp.int32, (8, 128), 1)
        self.lane = lane
        self.low = sub < 4
        self.top = (sub & 3) == 3
        self.bottom = (sub & 3) == 0
        self.lane_first = lane == 0
        self.lane_last = lane == 127
        self.last = jnp.logical_and(lane == 127, sub >= 4)
        self.marks = marks
        if marks is not None:
            self.even = marks[0] > 0.5
            self.copy0 = marks[1] > 0.5

    def above(self, x):
        return jnp.where(self.top, 0.0, pltpu.roll(x, 7, 0))

    def below(self, x):
        return jnp.where(self.bottom, 0.0, pltpu.roll(x, 1, 0))

    def before(self, x):
        r = pltpu.roll(x, 1, 1)
        return jnp.where(self.lane_first, jnp.where(self.low, 0.0, pltpu.roll(r, 4, 0)), r)

    def after(self, x, end):
        r = pltpu.roll(x, 127, 1)
        return jnp.where(self.lane_last, jnp.where(self.low, pltpu.roll(r, 4, 0), end), r)

    def pick(self, x, y):
        return jnp.where(self.even, x, y)


def apply_operator(mv, u_ref, coeff, y_ref, acc_ref, up_ref):
    for b in range(N):
        for c in range(N):
            u = [u_ref[at(a, b, c)] for a in range(4)]
            u.append(mv.above(u[0]))
            up_ref[b * 5 + c] = u[4]
            for a, value in enumerate(line(u)):
                acc_ref[at(a, b, c)] = value
    for a in (4, 0, 1, 2, 3):
        scale = {}
        for b in range(3):
            for c in range(b, 3):
                scale[b, c] = scale[c, b] = coeff * weight(a, b, c)
        u = [[up_ref[b * 5 + c] if a == 4 else u_ref[at(a, b, c)] for c in range(N)] for b in range(N)]
        across = [line([u[b][c] for b in range(N)]) for c in range(N)]
        for b in range(N):
            along = line(u[b])
            y = [(acc_ref[at(a, b, c)] + along[c] + across[c][b]) * scale[SYM[b], SYM[c]] for c in range(N)]
            if a == 4:
                for c in range(N):
                    up_ref[b * 5 + c] = y[c]
                continue
            if a == 0:
                y = [y[c] + mv.below(up_ref[b * 5 + c]) for c in range(N)]
            y[0] = y[0] + mv.before(y[4])
            for c in range(N):
                y_ref[at(a, b, c)] = y[c]


def put_faces(mv, y_ref, a_ref, b_ref, first=0):
    ends = [jnp.zeros((8, 128), F32)] * 2
    for a in range(4):
        for c in range(4):
            low, high = y_ref[at(a, 0, c)], y_ref[at(a, 4, c)]
            a_ref[first + a * 4 + c] = mv.pick(high, low)
            b_ref[first + a * 4 + c] = mv.pick(low, high)
        for side in range(2):
            ends[side] = jnp.where(mv.lane == a, pltpu.roll(y_ref[at(a, 4 * side, 4)], a + 1, 1), ends[side])
    a_ref[first + 16] = mv.pick(ends[1], ends[0])
    b_ref[first + 16] = mv.pick(ends[0], ends[1])


def got_faces(mv, a_ref, b_ref, count, a_first=0, b_first=0):
    has_left, has_right = mv.marks[2], mv.marks[3]
    left, right = [], []
    for k in range(count):
        x, y = a_ref[a_first + k], b_ref[b_first + k]
        left.append(mv.pick(y, x) * has_left)
        right.append(mv.pick(x, y) * has_right)
    out = []
    for v in (left, right):
        rows = []
        for a in range(4):
            rows.extend(v[a * 4 : a * 4 + 4])
            rows.append(pltpu.roll(v[16], 127 - a, 1))
        out.append(rows + v[17:])
    return out


def inverse_at(inv_ref, a, b, c):
    kind = (0 if a == 0 else 6) + (0 if b == 0 else 4 if b == 4 else 2) + (0 if c == 0 else 1)
    return inv_ref[kind] * inverse_factor(a, b, c)


def residual_row(mv, f_ref, y_ref, left, right, a, b):
    row = []
    for c in range(N):
        r = f_ref[at(a, b, c)] - y_ref[at(a, b, c)]
        if b == 0:
            r = r - left[a * 5 + c]
        if b == 4:
            r = r - right[a * 5 + c]
        row.append(r)
    return row


def smooth(mv, u_ref, f_ref, y_ref, left, right, inv_ref, out_ref):
    for a in range(4):
        for b in range(N):
            r = residual_row(mv, f_ref, y_ref, left, right, a, b)
            u = [u_ref[at(a, b, c)] + r[c] * inverse_at(inv_ref, a, b, c) for c in range(N)]
            u[4] = mv.after(u[0], u[4])
            for c in range(N):
                out_ref[at(a, b, c)] = u[c]


def half_rows(mv, ref, out_ref):
    def turned(x):
        return jnp.where(mv.copy0, x, pltpu.roll(x, 4, 0))

    ends = jnp.zeros((8, 128), F32)
    for k in range(20):
        for c in (0, 2):
            x, y = turned(ref[5 * k + c]), turned(ref[5 * k + c + 1])
            out_ref[pl.ds(16 * k + 4 * c, 8)] = jnp.where(mv.low, x, pltpu.roll(y, 4, 0))
        ends = jnp.where(mv.lane == k, pltpu.roll(turned(ref[5 * k + 4]), k + 1, 1), ends)
    out_ref[pl.ds(320, 8)] = ends


def pack_kernel(load_ref, out_ref, sum_ref):
    row = lax.broadcasted_iota(jnp.int32, (100, 128), 0)
    sum_ref[pl.ds(0, 100)] = load_ref[pl.ds(0, 100)] + jnp.where((row & 3) == 0, 0.0, load_ref[pl.ds(399, 100)])
    sum_ref[pl.ds(100, 404)] = load_ref[pl.ds(100, 404)]
    row = lax.broadcasted_iota(jnp.int32, (16, 128), 0)
    lane = lax.broadcasted_iota(jnp.int32, (16, 128), 1)
    moved = jnp.logical_and(row < 4, lane > 0)
    ends = jnp.zeros((16, 128), F32)
    for k in range(20):
        x = sum_ref[pl.ds(20 * k + 16, 16)]
        out_ref[pl.ds(16 * k, 16)] = sum_ref[pl.ds(20 * k, 16)] + jnp.where(moved, pltpu.roll(x, 1, 1), 0.0)
        ends = jnp.where(lane == k, pltpu.roll(x, k + 1, 1), ends)
    out_ref[pl.ds(320, 4)] = ends[:4]
    out_ref[pl.ds(324, 4)] = load_ref[pl.ds(500, 4)]


def unpack_kernel(marks, same_ref, other_ref, f_ref, coeff_ref, a_ref, b_ref):
    mv = Moves(marks)

    def pair(n):
        x, y = same_ref[pl.ds(4 * n, 8)], other_ref[pl.ds(4 * n, 8)]
        h0, h1 = jnp.where(mv.copy0, x, y), jnp.where(mv.copy0, y, x)
        return jnp.where(mv.low, h0, pltpu.roll(h1, 4, 0)), jnp.where(mv.low, pltpu.roll(h0, 4, 0), h1)

    ends, coeff = pair(80)
    coeff_ref[...] = coeff
    joint = jnp.logical_and(mv.lane_first, jnp.logical_not(mv.low))
    for k in range(20):
        for c in (0, 2):
            f_ref[5 * k + c], f_ref[5 * k + c + 1] = pair(4 * k + c)
        over = pltpu.roll(pltpu.roll(ends, (128 - k) % 128, 1), 4, 0)
        f_ref[5 * k] = f_ref[5 * k] + jnp.where(joint, over, 0.0)
        f_ref[5 * k + 4] = pltpu.roll(ends, 127 - k, 1)
    put_faces(mv, f_ref, a_ref, b_ref)
    a_ref[17] = coeff
    b_ref[17] = coeff


def first_kernel(marks, part_ref, coeff_ref, ga_ref, gb_ref, u_ref, y_ref, f_ref, inv_ref, a_ref, b_ref, acc_ref, up_ref):
    mv = Moves(marks)
    left, right = got_faces(mv, ga_ref, gb_ref, 18)
    coeff = coeff_ref[...]
    for kind_b, value in enumerate((coeff + left[20], coeff, coeff + right[20])):
        for kind_a, v in enumerate((value + mv.below(value), value)):
            inv_ref[kind_a * 6 + kind_b * 2] = 1.0 / (v + mv.before(v))
            inv_ref[kind_a * 6 + kind_b * 2 + 1] = 1.0 / v
    for a in range(4):
        for b in range(N):
            f = [part_ref[at(a, b, c)] for c in range(N)]
            if b == 0:
                f = [f[c] + left[a * 5 + c] for c in range(N)]
            if b == 4:
                f = [f[c] + right[a * 5 + c] for c in range(N)]
            u = [f[c] * inverse_at(inv_ref, a, b, c) for c in range(N)]
            u[4] = mv.after(u[0], u[4])
            for c in range(N):
                f_ref[at(a, b, c)] = f[c]
                u_ref[at(a, b, c)] = u[c]
    apply_operator(mv, u_ref, coeff, y_ref, acc_ref, up_ref)
    put_faces(mv, y_ref, a_ref, b_ref)


def sweep_kernel(marks, u_ref, y_ref, f_ref, inv_ref, coeff_ref, ga_ref, gb_ref, un_ref, yn_ref, a_ref, b_ref, acc_ref, up_ref):
    mv = Moves(marks)
    left, right = got_faces(mv, ga_ref, gb_ref, 17)
    smooth(mv, u_ref, f_ref, y_ref, left, right, inv_ref, un_ref)
    apply_operator(mv, un_ref, coeff_ref[...], yn_ref, acc_ref, up_ref)
    put_faces(mv, yn_ref, a_ref, b_ref)


def last_sweep_kernel(marks, u_ref, y_ref, f_ref, inv_ref, coeff_ref, ga_ref, gb_ref, yn_ref, a_ref, b_ref, half_ref, un_ref, acc_ref, up_ref):
    sweep_kernel(marks, u_ref, y_ref, f_ref, inv_ref, coeff_ref, ga_ref, gb_ref, un_ref, yn_ref, a_ref, b_ref, acc_ref, up_ref)
    half_rows(Moves(marks), un_ref, half_ref)


def restrict_kernel(marks, u_ref, y_ref, f_ref, inv_ref, coeff_ref, ga_ref, gb_ref, part_ref, un_ref, own_ref, a_ref, b_ref, yn_ref, acc_ref, up_ref):
    mv = Moves(marks)
    left, right = got_faces(mv, ga_ref, gb_ref, 17)
    smooth(mv, u_ref, f_ref, y_ref, left, right, inv_ref, un_ref)
    apply_operator(mv, un_ref, coeff_ref[...], yn_ref, acc_ref, up_ref)
    put_faces(mv, yn_ref, a_ref, b_ref, 5)
    z = [[], []]
    for c in range(N):
        rows = [[], []]
        for a in range(4):
            r = [part_ref[at(a, b, c)] - yn_ref[at(a, b, c)] for b in range(N)]
            inner = [sum(float(INTERP[b, side]) * r[b] for b in (1, 2, 3)) for side in range(2)]
            rows[0].append(r[0] + inner[0])
            rows[1].append(r[4] + inner[1])
        for side in range(2):
            x = rows[side]
            low = x[0] + sum(float(INTERP[a, 0]) * x[a] for a in (1, 2, 3))
            z[side].append(low + mv.below(sum(float(INTERP[a, 1]) * x[a] for a in (1, 2, 3))))
    for side in range(2):
        x = z[side]
        inner = [sum(float(INTERP[c, k]) * x[c] for c in (1, 2, 3)) for k in range(2)]
        own_ref[side * 2] = x[0] + inner[0] + mv.before(inner[1])
        own_ref[side * 2 + 1] = jnp.where(mv.last, x[4] + inner[1], 0.0)
    own_ref[4] = coeff_ref[...]
    for k in range(5):
        a_ref[k] = own_ref[k]


def chip_kernel(marks, own_ref, ga_ref, b_ref, chip_ref, near_ref):
    mv = Moves(marks)
    for k in range(5):
        x, y = own_ref[k], ga_ref[k]
        low, high = mv.pick(x, y), mv.pick(y, x)
        chip_ref[k] = low
        chip_ref[5 + k] = high
        near_ref[k] = low
        near_ref[5 + k] = high
    for k in range(17):
        near_ref[10 + k] = b_ref[5 + k]


def side_kernel(near_ref, second_ref, third_ref, out_ref):
    for k in range(10):
        out_ref[k] = near_ref[k]
        out_ref[10 + k] = second_ref[k]
        out_ref[20 + k] = third_ref[k]


def coarse_solve(mv, chip_ref, mine_ref, other_ref):
    window = []
    for w in range(WIN):
        rows = []
        ok = mv.marks[4 + w]
        for k in range(5):
            if w in (6, 7):
                rows.append(chip_ref[(w - 6) * 5 + k])
                continue
            if w < 6:
                slot = (2 - w // 2) * 10 + (w % 2) * 5 + k
                x = mv.pick(mine_ref[slot], other_ref[slot])
            else:
                slot = (w // 2 - 4) * 10 + (w % 2) * 5 + k
                x = mv.pick(other_ref[slot], mine_ref[slot])
            rows.append(x * ok)
        window.append(rows)
    coeffs = [rows[4] for rows in window]
    load, inverse, value = {}, {}, {}
    factor = COARSE_RELAX / (2.0 / 3.0)
    for j in range(2, 13):
        load[j] = [window[j - 1][2 + g] + window[j][g] for g in range(2)]
        k = coeffs[j - 1] + coeffs[j]
        k = k + mv.below(k)
        inverse[j] = [jnp.where(v > 0.0, factor / v, 0.0) for v in (k + mv.before(k), k)]
        value[j] = [inverse[j][g] * load[j][g] for g in range(2)]
    for step in range(NC - 1):
        first, final = 2 + step, 12 - step
        nodes = {}
        for j in range(first, final + 1):
            value[j][1] = mv.after(value[j][0], value[j][1])
            nodes[j] = [value[j], [mv.above(v) for v in value[j]]]
        sums = {j: [[None, None], [None, None]] for j in range(first, final + 1)}
        for j in range(first, final):
            v = {(a, b, c): nodes[j + b][a][c] for a in range(2) for b in range(2) for c in range(2)}
            for axis in range(3):
                v = butterfly(v, axis)
            cf = [coeffs[j] * 0.125, coeffs[j] * (0.125 * 2.0 / 3.0), coeffs[j] * (0.125 / 3.0)]
            v = {key: None if sum(key) == 0 else x * cf[sum(key) - 1] for key, x in v.items()}
            for axis in range(3):
                v = butterfly(v, axis)
            for (a, b, c), x in v.items():
                old = sums[j + b][a][c]
                sums[j + b][a][c] = x if old is None else old + x
        new = {}
        for j in range(first + 1, final):
            s = sums[j]
            row = [s[0][c] + mv.below(s[1][c]) for c in range(2)]
            row[0] = row[0] + mv.before(row[1])
            new[j] = [value[j][g] + inverse[j][g] * (load[j][g] - row[g]) for g in range(2)]
        value = new
    for j in value:
        value[j][1] = mv.after(value[j][0], value[j][1])
    lines = [[mv.pick(value[5 + m][g], value[6 + m][g]) for g in range(2)] for m in range(4)]
    return lines, mv.pick(coeffs[5], coeffs[6]), mv.pick(coeffs[7], coeffs[8])


def butterfly(v, axis):
    out = {}
    for key in v:
        if key[axis]:
            continue
        up = tuple(1 if k == axis else key[k] for k in range(3))
        x, y = v[key], v[up]
        out[key] = y if x is None else x + y
        out[up] = -y if x is None else x - y
    return out


def nodal(mv, pair, count):
    rows = []
    up = [mv.above(v) for v in pair]
    for a in range(count):
        lo, hi = float(INTERP[a, 0]), float(INTERP[a, 1])
        if a == 0:
            ends = pair
        elif a == 4:
            ends = up
        else:
            ends = [lo * pair[g] + hi * up[g] for g in range(2)]
        rows.append([ends[0] if c == 0 else ends[1] if c == 4 else float(INTERP[c, 0]) * ends[0] + float(INTERP[c, 1]) * ends[1] for c in range(N)])
    return rows


def neighbour_face(mv, near, far, coeff):
    w = [float(x) for x in weights]
    x = nodal(mv, near, N)
    z = nodal(mv, far, N)
    y = []
    for a in range(N):
        row = []
        for c in range(N):
            v = (x[a][c] - z[a][c]) * (0.5 * weight(a, c))
            if a in (0, 4):
                v = v + (x[a][c] - x[4 - a][c]) * (0.5 * w[0] * w[SYM[c]])
            if c in (0, 4):
                v = v + (x[a][c] - x[a][4 - c]) * (0.5 * w[0] * w[SYM[a]])
            row.append(v * coeff)
        y.append(row)
    out = []
    for a in range(4):
        row = [y[0][c] + mv.below(y[4][c]) for c in range(N)] if a == 0 else y[a]
        row[0] = row[0] + mv.before(row[4])
        out.extend(row)
    return out


def correct_kernel(marks, u_ref, f_ref, inv_ref, coeff_ref, ga_ref, near_ref, chip_ref, mine_ref, other_ref, un_ref, yn_ref, a_ref, b_ref, ua_ref, ya_ref, face_ref, acc_ref, up_ref):
    mv = Moves(marks)
    coeff = coeff_ref[...]
    lines, coeff_left, coeff_right = coarse_solve(mv, chip_ref, mine_ref, other_ref)
    for k, v in enumerate(neighbour_face(mv, lines[1], lines[0], coeff_left)):
        face_ref[k] = v
    for k, v in enumerate(neighbour_face(mv, lines[2], lines[3], coeff_right)):
        face_ref[20 + k] = v
    low, high = nodal(mv, lines[1], 4), nodal(mv, lines[2], 4)
    for a in range(4):
        for b in range(N):
            for c in range(N):
                if b == 0:
                    v = low[a][c]
                elif b == 4:
                    v = high[a][c]
                else:
                    v = float(INTERP[b, 0]) * low[a][c] + float(INTERP[b, 1]) * high[a][c]
                ua_ref[at(a, b, c)] = u_ref[at(a, b, c)] + v
    apply_operator(mv, ua_ref, coeff, ya_ref, acc_ref, up_ref)
    left, right = got_faces(mv, ga_ref, near_ref, 17, 5, 10)
    left = [left[k] + face_ref[k] for k in range(20)]
    right = [right[k] + face_ref[20 + k] for k in range(20)]
    smooth(mv, ua_ref, f_ref, ya_ref, left, right, inv_ref, un_ref)
    apply_operator(mv, un_ref, coeff, yn_ref, acc_ref, up_ref)
    put_faces(mv, yn_ref, a_ref, b_ref)


def residual_kernel(marks, y_ref, f_ref, ga_ref, gb_ref, half_ref, r_ref):
    mv = Moves(marks)
    left, right = got_faces(mv, ga_ref, gb_ref, 17)
    for a in range(4):
        for b in range(N):
            r = residual_row(mv, f_ref, y_ref, left, right, a, b)
            r[4] = mv.after(r[0], r[4])
            for c in range(N):
                r_ref[at(a, b, c)] = r[c]
    half_rows(mv, r_ref, half_ref)


def spread_kernel(half_ref, out_ref):
    lane = lax.broadcasted_iota(jnp.int32, (8, 128), 1)
    ends = half_ref[pl.ds(320, 8)]
    for k in range(20):
        out_ref[pl.ds(20 * k, 16)] = half_ref[pl.ds(16 * k, 16)]
        last = jnp.where(lane == 127, pltpu.roll(ends, 127 - k, 1), pltpu.roll(half_ref[pl.ds(16 * k, 8)], 127, 1))
        out_ref[pl.ds(20 * k + 16, 4)] = last[:4]
    row = lax.broadcasted_iota(jnp.int32, (100, 128), 0)
    out_ref[pl.ds(400, 100)] = jnp.where((row & 3) == 3, 0.0, out_ref[pl.ds(1, 100)])


VM = pl.BlockSpec(memory_space=pltpu.VMEM)
FIELD = (100, 8, 128)
WORK = [(125, 8, 128), (25, 8, 128)]


def call(name, kernel, outs, scratch, *args):
    return pl.pallas_call(
        kernel,
        out_shape=[jax.ShapeDtypeStruct(s, F32) for s in outs],
        in_specs=[VM] * len(args),
        out_specs=[VM] * len(outs),
        scratch_shapes=[pltpu.VMEM(s, F32) for s in scratch],
        compiler_params=pltpu.CompilerParams(vmem_limit_bytes=12 * 1024 * 1024),
        name=name,
    )(*args)


def placement(sizes):
    _, ey, lin = sizes
    place = list(range(ey * lin))
    if lin == 64:
        for s in place[:]:
            side, p, y, core = s // 64, s // 8 % 8, s // 2 % 4, s % 2
            z = (p - side) % 8
            place[s] = side * 64 + z * 8 + (3 - y if p % 2 else y) * 2 + core
    return place


def per_device(sizes):
    strips = sizes[1] * sizes[2]
    chips = strips // 2
    place = placement(sizes)
    device = [[copy * strips + place[s] for s in range(strips)] for copy in range(2)]
    to_same = [(e * strips + s, device[e][s]) for e in range(2) for s in range(strips)]
    to_other = [(e * strips + s, device[1 - e][s]) for e in range(2) for s in range(strips)]
    back = [(b, a) for a, b in to_same]
    within = [(device[e][s], device[e][s ^ 1]) for e in range(2) for s in range(strips)]

    def chip_pairs(d):
        pairs = []
        for e in range(2):
            for s in range(strips):
                k = s // 2 - d if s % 2 == 0 else s // 2 + d
                if 0 <= k < chips:
                    pairs.append((device[e][s], device[e][2 * k + 1 - s % 2]))
                else:
                    pairs.append((device[e][s], device[1 - e][s]))
        return pairs

    beyond = {d: chip_pairs(d) for d in (1, 2, 3)}
    table = np.zeros((2 * strips, 4 + WIN), np.float32)
    for copy in range(2):
        for s in range(strips):
            window = [0 <= s - s % 2 - 6 + w < strips for w in range(WIN)]
            table[device[copy][s]] = [s % 2 == 0, copy == 0, s > 0, s < strips - 1, *window]

    def swap(x, pairs):
        return lax.ppermute(x, AXES, pairs)

    def restore(x):
        return x if place == sorted(place) else swap(x, back)

    def run(load, kappa, wet):
        marks = lax.dynamic_index_in_dim(jnp.asarray(table), lax.axis_index(AXES), 0, keepdims=False)
        marks = jnp.broadcast_to(marks[:, None, None], (4 + WIN, 8, 128))
        coeff = kappa * jnp.where(wet == 1, 1.0, 0.05).astype(F32)
        packed = jnp.concatenate([load.reshape(500, 1, 128), coeff.reshape(4, 1, 128)]).reshape(504, 128)
        (packed,) = call("pack", pack_kernel, [(328, 128)], [(504, 128)], packed)
        same, other = packed if place == sorted(place) else swap(packed, to_same), swap(packed, to_other)
        part, coeff, a, b = call("unpack", unpack_kernel, [FIELD, (8, 128), (18, 8, 128), (18, 8, 128)], [], marks, same, other)
        faces = [(17, 8, 128), (17, 8, 128)]

        def trade(a, b):
            return swap(a, within), swap(b, beyond[1])

        a, b = trade(a, b)
        u, y, f, inv, a, b = call("first", first_kernel, [FIELD, FIELD, FIELD, (12, 8, 128), *faces], WORK, marks, part, coeff, a, b)

        def sweep(u, y, a, b):
            a, b = trade(a, b)
            return call("sweep", sweep_kernel, [FIELD, FIELD, *faces], WORK, marks, u, y, f, inv, coeff, a, b)

        def sweep_and_correct(u, y, a, b):
            a, b = trade(a, b)
            u, own, a, b = call("restrict", restrict_kernel, [FIELD, (5, 8, 128), (22, 8, 128), (22, 8, 128)], [FIELD, *WORK], marks, u, y, f, inv, coeff, a, b, part)
            a = swap(a, within)
            chip, near = call("chip", chip_kernel, [(10, 8, 128), (27, 8, 128)], [], marks, own, a, b)
            near, second, third = swap(near, beyond[1]), swap(chip, beyond[2]), swap(chip, beyond[3])
            (mine,) = call("side", side_kernel, [(30, 8, 128)], [], near, second, third)
            theirs = swap(mine, within)
            return call("correct", correct_kernel, [FIELD, FIELD, *faces], [FIELD, FIELD, (40, 8, 128), *WORK], marks, u, f, inv, coeff, a, near, chip, mine, theirs)

        u, y, a, b = sweep_and_correct(u, y, a, b)
        u, y, a, b = sweep(u, y, a, b)
        u, y, a, b = sweep(u, y, a, b)
        u, y, a, b = sweep_and_correct(u, y, a, b)
        a, b = trade(a, b)
        y, a, b, half = call("last", last_sweep_kernel, [FIELD, *faces, (328, 128)], [FIELD, *WORK], marks, u, y, f, inv, coeff, a, b)
        a, b = trade(a, b)
        half = restore(half)
        (left_half,) = call("residual", residual_kernel, [(328, 128)], [FIELD], marks, y, f, a, b)
        (solved,) = call("spread", spread_kernel, [(500, 128)], [], half)
        (rest,) = call("spread", spread_kernel, [(500, 128)], [], restore(left_half))
        return solved.reshape(load.shape), rest.reshape(load.shape)

    return run


def solution(mesh):
    sizes = tuple(mesh.shape[name] for name in AXES)
    whole = P(None, None, None, None, ("ey", "lin"), "ex")
    flat = P(None, ("ey", "lin"), "ex")
    return jax.shard_map(per_device(sizes), mesh=mesh, in_specs=(whole, flat, flat), out_specs=(whole, whole), check_vma=False)
```

```python
import math

import jax
import jax.numpy as jnp
import numpy as np
from jax import lax
from jax.experimental import pallas as pl
from jax.experimental.pallas import tpu as pltpu
from jax.sharding import PartitionSpec as P

AXES = ("ex", "ey", "lin")
N = 5
NC = 4
WIN = 14
FINE_RELAX = 0.25
COARSE_RELAX = 0.4
F32 = jnp.float32

points = np.array([-1.0, -math.sqrt(3.0 / 7.0), 0.0, math.sqrt(3.0 / 7.0), 1.0])
weights = np.array([0.1, 49.0 / 90.0, 32.0 / 45.0, 49.0 / 90.0, 0.1])


def stiffness():
    eye = np.eye(N)
    spread = points[:, None] - points[None, :] + eye
    factors = np.prod(spread, axis=1)
    deriv = factors[:, None] / (factors[None, :] * spread)
    deriv = np.where(eye > 0, (np.sum(1.0 / spread, axis=1) - 1.0)[:, None], deriv)
    return deriv.T @ (weights[:, None] * deriv)


STIFF = stiffness()
LINE = STIFF / weights[:, None]
EVEN = [[float(LINE[i, j] + LINE[i, 4 - j]) / 2 for j in range(2)] for i in range(3)]
ODD = [[float(LINE[i, j] - LINE[i, 4 - j]) / 2 for j in range(2)] for i in range(2)]
INTERP = np.stack([(1.0 - points) / 2.0, (1.0 + points) / 2.0], axis=1)
SYM = [0, 1, 2, 1, 0]


def weight(*nodes):
    return float(np.prod([weights[SYM[k]] for k in sorted(SYM[n] for n in nodes)]))


def inverse_factor(a, b, c):
    s, w = np.diag(STIFF), weights
    a, b, c = sorted(SYM[n] for n in (a, b, c))
    return FINE_RELAX / float(s[a] * w[b] * w[c] + w[a] * s[b] * w[c] + w[a] * w[b] * s[c])


def at(a, b, c):
    return a * 25 + b * 5 + c


def line(u):
    m2 = u[2] + u[2]
    e0, e1 = u[0] + u[4] - m2, u[1] + u[3] - m2
    o0, o1 = u[0] - u[4], u[1] - u[3]
    even = [EVEN[i][0] * e0 + EVEN[i][1] * e1 for i in range(3)]
    odd = [ODD[i][0] * o0 + ODD[i][1] * o1 for i in range(2)]
    return [even[0] + odd[0], even[1] + odd[1], even[2], even[1] - odd[1], even[0] - odd[0]]


class Moves:
    def __init__(self, marks=None):
        sub = lax.broadcasted_iota(jnp.int32, (8, 128), 0)
        lane = lax.broadcasted_iota(jnp.int32, (8, 128), 1)
        self.lane = lane
        self.low = sub < 4
        self.top = (sub & 3) == 3
        self.bottom = (sub & 3) == 0
        self.lane_first = lane == 0
        self.lane_last = lane == 127
        self.last = jnp.logical_and(lane == 127, sub >= 4)
        self.marks = marks
        if marks is not None:
            self.even = marks[0] > 0.5
            self.copy0 = marks[1] > 0.5

    def above(self, x):
        return jnp.where(self.top, 0.0, pltpu.roll(x, 7, 0))

    def below(self, x):
        return jnp.where(self.bottom, 0.0, pltpu.roll(x, 1, 0))

    def before(self, x):
        r = pltpu.roll(x, 1, 1)
        return jnp.where(self.lane_first, jnp.where(self.low, 0.0, pltpu.roll(r, 4, 0)), r)

    def after(self, x, end):
        r = pltpu.roll(x, 127, 1)
        return jnp.where(self.lane_last, jnp.where(self.low, pltpu.roll(r, 4, 0), end), r)

    def pick(self, x, y):
        return jnp.where(self.even, x, y)


def apply_operator(mv, u_ref, coeff, y_ref, acc_ref, up_ref):
    for b in range(N):
        for c in range(N):
            u = [u_ref[at(a, b, c)] for a in range(4)]
            u.append(mv.above(u[0]))
            up_ref[b * 5 + c] = u[4]
            for a, value in enumerate(line(u)):
                acc_ref[at(a, b, c)] = value
    for a in (4, 0, 1, 2, 3):
        scale = {}
        for b in range(3):
            for c in range(b, 3):
                scale[b, c] = scale[c, b] = coeff * weight(a, b, c)
        u = [[up_ref[b * 5 + c] if a == 4 else u_ref[at(a, b, c)] for c in range(N)] for b in range(N)]
        across = [line([u[b][c] for b in range(N)]) for c in range(N)]
        for b in range(N):
            along = line(u[b])
            y = [(acc_ref[at(a, b, c)] + along[c] + across[c][b]) * scale[SYM[b], SYM[c]] for c in range(N)]
            if a == 4:
                for c in range(N):
                    up_ref[b * 5 + c] = y[c]
                continue
            if a == 0:
                y = [y[c] + mv.below(up_ref[b * 5 + c]) for c in range(N)]
            y[0] = y[0] + mv.before(y[4])
            for c in range(N):
                y_ref[at(a, b, c)] = y[c]


def put_faces(mv, y_ref, a_ref, b_ref, first=0):
    ends = [jnp.zeros((8, 128), F32)] * 2
    for a in range(4):
        for c in range(4):
            low, high = y_ref[at(a, 0, c)], y_ref[at(a, 4, c)]
            a_ref[first + a * 4 + c] = mv.pick(high, low)
            b_ref[first + a * 4 + c] = mv.pick(low, high)
        for side in range(2):
            ends[side] = jnp.where(mv.lane == a, pltpu.roll(y_ref[at(a, 4 * side, 4)], a + 1, 1), ends[side])
    a_ref[first + 16] = mv.pick(ends[1], ends[0])
    b_ref[first + 16] = mv.pick(ends[0], ends[1])


def got_faces(mv, a_ref, b_ref, count, a_first=0, b_first=0):
    has_left, has_right = mv.marks[2], mv.marks[3]
    left, right = [], []
    for k in range(count):
        x, y = a_ref[a_first + k], b_ref[b_first + k]
        left.append(mv.pick(y, x) * has_left)
        right.append(mv.pick(x, y) * has_right)
    out = []
    for v in (left, right):
        rows = []
        for a in range(4):
            rows.extend(v[a * 4 : a * 4 + 4])
            rows.append(pltpu.roll(v[16], 127 - a, 1))
        out.append(rows + v[17:])
    return out


def inverse_at(inv_ref, a, b, c):
    kind = (0 if a == 0 else 6) + (0 if b == 0 else 4 if b == 4 else 2) + (0 if c == 0 else 1)
    return inv_ref[kind] * inverse_factor(a, b, c)


def residual_row(mv, f_ref, y_ref, left, right, a, b):
    row = []
    for c in range(N):
        r = f_ref[at(a, b, c)] - y_ref[at(a, b, c)]
        if b == 0:
            r = r - left[a * 5 + c]
        if b == 4:
            r = r - right[a * 5 + c]
        row.append(r)
    return row


def smooth(mv, u_ref, f_ref, y_ref, left, right, inv_ref, out_ref):
    for a in range(4):
        for b in range(N):
            r = residual_row(mv, f_ref, y_ref, left, right, a, b)
            u = [u_ref[at(a, b, c)] + r[c] * inverse_at(inv_ref, a, b, c) for c in range(N)]
            u[4] = mv.after(u[0], u[4])
            for c in range(N):
                out_ref[at(a, b, c)] = u[c]


def half_rows(mv, ref, out_ref):
    def turned(x):
        return jnp.where(mv.copy0, x, pltpu.roll(x, 4, 0))

    ends = jnp.zeros((8, 128), F32)
    for k in range(20):
        for c in (0, 2):
            x, y = turned(ref[5 * k + c]), turned(ref[5 * k + c + 1])
            out_ref[pl.ds(16 * k + 4 * c, 8)] = jnp.where(mv.low, x, pltpu.roll(y, 4, 0))
        ends = jnp.where(mv.lane == k, pltpu.roll(turned(ref[5 * k + 4]), k + 1, 1), ends)
    out_ref[pl.ds(320, 8)] = ends


def pack_kernel(load_ref, out_ref, sum_ref):
    row = lax.broadcasted_iota(jnp.int32, (100, 128), 0)
    sum_ref[pl.ds(0, 100)] = load_ref[pl.ds(0, 100)] + jnp.where((row & 3) == 0, 0.0, load_ref[pl.ds(399, 100)])
    sum_ref[pl.ds(100, 404)] = load_ref[pl.ds(100, 404)]
    row = lax.broadcasted_iota(jnp.int32, (16, 128), 0)
    lane = lax.broadcasted_iota(jnp.int32, (16, 128), 1)
    moved = jnp.logical_and(row < 4, lane > 0)
    ends = jnp.zeros((16, 128), F32)
    for k in range(20):
        x = sum_ref[pl.ds(20 * k + 16, 16)]
        out_ref[pl.ds(16 * k, 16)] = sum_ref[pl.ds(20 * k, 16)] + jnp.where(moved, pltpu.roll(x, 1, 1), 0.0)
        ends = jnp.where(lane == k, pltpu.roll(x, k + 1, 1), ends)
    out_ref[pl.ds(320, 4)] = ends[:4]
    out_ref[pl.ds(324, 4)] = load_ref[pl.ds(500, 4)]


def unpack_kernel(marks, same_ref, other_ref, f_ref, coeff_ref, a_ref, b_ref):
    mv = Moves(marks)

    def pair(n):
        x, y = same_ref[pl.ds(4 * n, 8)], other_ref[pl.ds(4 * n, 8)]
        h0, h1 = jnp.where(mv.copy0, x, y), jnp.where(mv.copy0, y, x)
        return jnp.where(mv.low, h0, pltpu.roll(h1, 4, 0)), jnp.where(mv.low, pltpu.roll(h0, 4, 0), h1)

    ends, coeff = pair(80)
    coeff_ref[...] = coeff
    joint = jnp.logical_and(mv.lane_first, jnp.logical_not(mv.low))
    for k in range(20):
        for c in (0, 2):
            f_ref[5 * k + c], f_ref[5 * k + c + 1] = pair(4 * k + c)
        over = pltpu.roll(pltpu.roll(ends, (128 - k) % 128, 1), 4, 0)
        f_ref[5 * k] = f_ref[5 * k] + jnp.where(joint, over, 0.0)
        f_ref[5 * k + 4] = pltpu.roll(ends, 127 - k, 1)
    put_faces(mv, f_ref, a_ref, b_ref)
    a_ref[17] = coeff
    b_ref[17] = coeff


def first_kernel(marks, part_ref, coeff_ref, ga_ref, gb_ref, u_ref, y_ref, f_ref, inv_ref, a_ref, b_ref, acc_ref, up_ref):
    mv = Moves(marks)
    left, right = got_faces(mv, ga_ref, gb_ref, 18)
    coeff = coeff_ref[...]
    for kind_b, value in enumerate((coeff + left[20], coeff, coeff + right[20])):
        for kind_a, v in enumerate((value + mv.below(value), value)):
            inv_ref[kind_a * 6 + kind_b * 2] = 1.0 / (v + mv.before(v))
            inv_ref[kind_a * 6 + kind_b * 2 + 1] = 1.0 / v
    for a in range(4):
        for b in range(N):
            f = [part_ref[at(a, b, c)] for c in range(N)]
            if b == 0:
                f = [f[c] + left[a * 5 + c] for c in range(N)]
            if b == 4:
                f = [f[c] + right[a * 5 + c] for c in range(N)]
            u = [f[c] * inverse_at(inv_ref, a, b, c) for c in range(N)]
            u[4] = mv.after(u[0], u[4])
            for c in range(N):
                f_ref[at(a, b, c)] = f[c]
                u_ref[at(a, b, c)] = u[c]
    apply_operator(mv, u_ref, coeff, y_ref, acc_ref, up_ref)
    put_faces(mv, y_ref, a_ref, b_ref)


def sweep_kernel(marks, u_ref, y_ref, f_ref, inv_ref, coeff_ref, ga_ref, gb_ref, un_ref, yn_ref, a_ref, b_ref, acc_ref, up_ref):
    mv = Moves(marks)
    left, right = got_faces(mv, ga_ref, gb_ref, 17)
    smooth(mv, u_ref, f_ref, y_ref, left, right, inv_ref, un_ref)
    apply_operator(mv, un_ref, coeff_ref[...], yn_ref, acc_ref, up_ref)
    put_faces(mv, yn_ref, a_ref, b_ref)


def last_sweep_kernel(marks, u_ref, y_ref, f_ref, inv_ref, coeff_ref, ga_ref, gb_ref, yn_ref, a_ref, b_ref, half_ref, un_ref, acc_ref, up_ref):
    sweep_kernel(marks, u_ref, y_ref, f_ref, inv_ref, coeff_ref, ga_ref, gb_ref, un_ref, yn_ref, a_ref, b_ref, acc_ref, up_ref)
    half_rows(Moves(marks), un_ref, half_ref)


def restrict_kernel(marks, u_ref, y_ref, f_ref, inv_ref, coeff_ref, ga_ref, gb_ref, part_ref, un_ref, yn_ref, own_ref, a_ref, b_ref, acc_ref, up_ref):
    mv = Moves(marks)
    left, right = got_faces(mv, ga_ref, gb_ref, 17)
    smooth(mv, u_ref, f_ref, y_ref, left, right, inv_ref, un_ref)
    apply_operator(mv, un_ref, coeff_ref[...], yn_ref, acc_ref, up_ref)
    put_faces(mv, yn_ref, a_ref, b_ref, 5)
    z = [[], []]
    for c in range(N):
        rows = [[], []]
        for a in range(4):
            r = [part_ref[at(a, b, c)] - yn_ref[at(a, b, c)] for b in range(N)]
            inner = [sum(float(INTERP[b, side]) * r[b] for b in (1, 2, 3)) for side in range(2)]
            rows[0].append(r[0] + inner[0])
            rows[1].append(r[4] + inner[1])
        for side in range(2):
            x = rows[side]
            low = x[0] + sum(float(INTERP[a, 0]) * x[a] for a in (1, 2, 3))
            z[side].append(low + mv.below(sum(float(INTERP[a, 1]) * x[a] for a in (1, 2, 3))))
    for side in range(2):
        x = z[side]
        inner = [sum(float(INTERP[c, k]) * x[c] for c in (1, 2, 3)) for k in range(2)]
        own_ref[side * 2] = x[0] + inner[0] + mv.before(inner[1])
        own_ref[side * 2 + 1] = jnp.where(mv.last, x[4] + inner[1], 0.0)
    own_ref[4] = coeff_ref[...]
    for k in range(5):
        a_ref[k] = own_ref[k]


def chip_kernel(marks, own_ref, ga_ref, b_ref, chip_ref, near_ref):
    mv = Moves(marks)
    for k in range(5):
        x, y = own_ref[k], ga_ref[k]
        low, high = mv.pick(x, y), mv.pick(y, x)
        chip_ref[k] = low
        chip_ref[5 + k] = high
        near_ref[k] = low
        near_ref[5 + k] = high
    for k in range(17):
        near_ref[10 + k] = b_ref[5 + k]


def side_kernel(near_ref, second_ref, third_ref, out_ref):
    for k in range(10):
        out_ref[k] = near_ref[k]
        out_ref[10 + k] = second_ref[k]
        out_ref[20 + k] = third_ref[k]


def coarse_solve(mv, chip_ref, mine_ref, other_ref):
    window = []
    for w in range(WIN):
        rows = []
        ok = mv.marks[4 + w]
        for k in range(5):
            if w in (6, 7):
                rows.append(chip_ref[(w - 6) * 5 + k])
                continue
            if w < 6:
                slot = (2 - w // 2) * 10 + (w % 2) * 5 + k
                x = mv.pick(mine_ref[slot], other_ref[slot])
            else:
                slot = (w // 2 - 4) * 10 + (w % 2) * 5 + k
                x = mv.pick(other_ref[slot], mine_ref[slot])
            rows.append(x * ok)
        window.append(rows)
    coeffs = [rows[4] for rows in window]
    load, inverse, value = {}, {}, {}
    factor = COARSE_RELAX / (2.0 / 3.0)
    for j in range(2, 13):
        load[j] = [window[j - 1][2 + g] + window[j][g] for g in range(2)]
        k = coeffs[j - 1] + coeffs[j]
        k = k + mv.below(k)
        inverse[j] = [jnp.where(v > 0.0, factor / v, 0.0) for v in (k + mv.before(k), k)]
        value[j] = [inverse[j][g] * load[j][g] for g in range(2)]
    for step in range(NC - 1):
        first, final = 2 + step, 12 - step
        nodes = {}
        for j in range(first, final + 1):
            value[j][1] = mv.after(value[j][0], value[j][1])
            nodes[j] = [value[j], [mv.above(v) for v in value[j]]]
        sums = {j: [[None, None], [None, None]] for j in range(first, final + 1)}
        for j in range(first, final):
            v = {(a, b, c): nodes[j + b][a][c] for a in range(2) for b in range(2) for c in range(2)}
            for axis in range(3):
                v = butterfly(v, axis)
            cf = [coeffs[j] * 0.125, coeffs[j] * (0.125 * 2.0 / 3.0), coeffs[j] * (0.125 / 3.0)]
            v = {key: None if sum(key) == 0 else x * cf[sum(key) - 1] for key, x in v.items()}
            for axis in range(3):
                v = butterfly(v, axis)
            for (a, b, c), x in v.items():
                old = sums[j + b][a][c]
                sums[j + b][a][c] = x if old is None else old + x
        new = {}
        for j in range(first + 1, final):
            s = sums[j]
            row = [s[0][c] + mv.below(s[1][c]) for c in range(2)]
            row[0] = row[0] + mv.before(row[1])
            new[j] = [value[j][g] + inverse[j][g] * (load[j][g] - row[g]) for g in range(2)]
        value = new
    for j in value:
        value[j][1] = mv.after(value[j][0], value[j][1])
    lines = [[mv.pick(value[5 + m][g], value[6 + m][g]) for g in range(2)] for m in range(4)]
    return lines, mv.pick(coeffs[5], coeffs[6]), mv.pick(coeffs[7], coeffs[8])


def butterfly(v, axis):
    out = {}
    for key in v:
        if key[axis]:
            continue
        up = tuple(1 if k == axis else key[k] for k in range(3))
        x, y = v[key], v[up]
        out[key] = y if x is None else x + y
        out[up] = -y if x is None else x - y
    return out


def nodal(mv, pair, count):
    rows = []
    up = [mv.above(v) for v in pair]
    for a in range(count):
        lo, hi = float(INTERP[a, 0]), float(INTERP[a, 1])
        if a == 0:
            ends = pair
        elif a == 4:
            ends = up
        else:
            ends = [lo * pair[g] + hi * up[g] for g in range(2)]
        rows.append([ends[0] if c == 0 else ends[1] if c == 4 else float(INTERP[c, 0]) * ends[0] + float(INTERP[c, 1]) * ends[1] for c in range(N)])
    return rows


def neighbour_face(mv, near, far, coeff):
    w = [float(x) for x in weights]
    x = nodal(mv, near, N)
    z = nodal(mv, far, N)
    y = []
    for a in range(N):
        row = []
        for c in range(N):
            v = (x[a][c] - z[a][c]) * (0.5 * weight(a, c))
            if a in (0, 4):
                v = v + (x[a][c] - x[4 - a][c]) * (0.5 * w[0] * w[SYM[c]])
            if c in (0, 4):
                v = v + (x[a][c] - x[a][4 - c]) * (0.5 * w[0] * w[SYM[a]])
            row.append(v * coeff)
        y.append(row)
    out = []
    for a in range(4):
        row = [y[0][c] + mv.below(y[4][c]) for c in range(N)] if a == 0 else y[a]
        row[0] = row[0] + mv.before(row[4])
        out.extend(row)
    return out


def add_correction(mv, low, high, coeff, u_ref, y_ref, ua_ref, ya_ref):
    half = coeff * 0.5
    found = {}

    def v(a, b, c):
        if (a, b, c) not in found:
            lo, hi = low[a][c], high[a][c]
            found[a, b, c] = lo if b == 0 else hi if b == 4 else float(INTERP[b, 0]) * lo + float(INTERP[b, 1]) * hi
        return found[a, b, c]

    def share(a, b, c):
        parts = []
        if a in (0, 4):
            parts.append((v(a, b, c) - v(4 - a, b, c)) * weight(b, c))
        if b in (0, 4):
            parts.append((v(a, b, c) - v(a, 4 - b, c)) * weight(a, c))
        if c in (0, 4):
            parts.append((v(a, b, c) - v(a, b, 4 - c)) * weight(a, b))
        return sum(parts[1:], parts[0]) * half if parts else None

    for a in range(4):
        for b in range(N):
            row = [share(a, b, c) for c in range(N)]
            if a == 0:
                for c in range(N):
                    under = share(4, b, c)
                    row[c] = row[c] + mv.below(under)
            row[0] = row[0] + mv.before(row[4])
            for c in range(N):
                ua_ref[at(a, b, c)] = u_ref[at(a, b, c)] + v(a, b, c)
                ya_ref[at(a, b, c)] = y_ref[at(a, b, c)] if row[c] is None else y_ref[at(a, b, c)] + row[c]


def correct_kernel(marks, u_ref, y_ref, f_ref, inv_ref, coeff_ref, ga_ref, near_ref, chip_ref, mine_ref, other_ref, un_ref, yn_ref, a_ref, b_ref, ua_ref, ya_ref, face_ref, acc_ref, up_ref):
    mv = Moves(marks)
    coeff = coeff_ref[...]
    lines, coeff_left, coeff_right = coarse_solve(mv, chip_ref, mine_ref, other_ref)
    for k, v in enumerate(neighbour_face(mv, lines[1], lines[0], coeff_left)):
        face_ref[k] = v
    for k, v in enumerate(neighbour_face(mv, lines[2], lines[3], coeff_right)):
        face_ref[20 + k] = v
    low, high = nodal(mv, lines[1], N), nodal(mv, lines[2], N)
    add_correction(mv, low, high, coeff, u_ref, y_ref, ua_ref, ya_ref)
    left, right = got_faces(mv, ga_ref, near_ref, 17, 5, 10)
    left = [left[k] + face_ref[k] for k in range(20)]
    right = [right[k] + face_ref[20 + k] for k in range(20)]
    smooth(mv, ua_ref, f_ref, ya_ref, left, right, inv_ref, un_ref)
    apply_operator(mv, un_ref, coeff, yn_ref, acc_ref, up_ref)
    put_faces(mv, yn_ref, a_ref, b_ref)


def residual_kernel(marks, y_ref, f_ref, ga_ref, gb_ref, half_ref, r_ref):
    mv = Moves(marks)
    left, right = got_faces(mv, ga_ref, gb_ref, 17)
    for a in range(4):
        for b in range(N):
            r = residual_row(mv, f_ref, y_ref, left, right, a, b)
            r[4] = mv.after(r[0], r[4])
            for c in range(N):
                r_ref[at(a, b, c)] = r[c]
    half_rows(mv, r_ref, half_ref)


def spread_kernel(half_ref, out_ref):
    lane = lax.broadcasted_iota(jnp.int32, (8, 128), 1)
    ends = half_ref[pl.ds(320, 8)]
    for k in range(20):
        out_ref[pl.ds(20 * k, 16)] = half_ref[pl.ds(16 * k, 16)]
        last = jnp.where(lane == 127, pltpu.roll(ends, 127 - k, 1), pltpu.roll(half_ref[pl.ds(16 * k, 8)], 127, 1))
        out_ref[pl.ds(20 * k + 16, 4)] = last[:4]
    row = lax.broadcasted_iota(jnp.int32, (100, 128), 0)
    out_ref[pl.ds(400, 100)] = jnp.where((row & 3) == 3, 0.0, out_ref[pl.ds(1, 100)])


VM = pl.BlockSpec(memory_space=pltpu.VMEM)
FIELD = (100, 8, 128)
WORK = [(125, 8, 128), (25, 8, 128)]


def call(name, kernel, outs, scratch, *args):
    return pl.pallas_call(
        kernel,
        out_shape=[jax.ShapeDtypeStruct(s, F32) for s in outs],
        in_specs=[VM] * len(args),
        out_specs=[VM] * len(outs),
        scratch_shapes=[pltpu.VMEM(s, F32) for s in scratch],
        compiler_params=pltpu.CompilerParams(vmem_limit_bytes=12 * 1024 * 1024),
        name=name,
    )(*args)


def placement(sizes):
    _, ey, lin = sizes
    place = list(range(ey * lin))
    if lin == 64:
        for s in place[:]:
            side, p, y, core = s // 64, s // 8 % 8, s // 2 % 4, s % 2
            z = (p - side) % 8
            place[s] = side * 64 + z * 8 + (3 - y if p % 2 else y) * 2 + core
    return place


def per_device(sizes):
    strips = sizes[1] * sizes[2]
    chips = strips // 2
    place = placement(sizes)
    device = [[copy * strips + place[s] for s in range(strips)] for copy in range(2)]
    to_same = [(e * strips + s, device[e][s]) for e in range(2) for s in range(strips)]
    to_other = [(e * strips + s, device[1 - e][s]) for e in range(2) for s in range(strips)]
    back = [(b, a) for a, b in to_same]
    within = [(device[e][s], device[e][s ^ 1]) for e in range(2) for s in range(strips)]

    def chip_pairs(d):
        pairs = []
        for e in range(2):
            for s in range(strips):
                k = s // 2 - d if s % 2 == 0 else s // 2 + d
                if 0 <= k < chips:
                    pairs.append((device[e][s], device[e][2 * k + 1 - s % 2]))
                else:
                    pairs.append((device[e][s], device[1 - e][s]))
        return pairs

    beyond = {d: chip_pairs(d) for d in (1, 2, 3)}
    table = np.zeros((2 * strips, 4 + WIN), np.float32)
    for copy in range(2):
        for s in range(strips):
            window = [0 <= s - s % 2 - 6 + w < strips for w in range(WIN)]
            table[device[copy][s]] = [s % 2 == 0, copy == 0, s > 0, s < strips - 1, *window]

    def swap(x, pairs):
        return lax.ppermute(x, AXES, pairs)

    def restore(x):
        return x if place == sorted(place) else swap(x, back)

    def run(load, kappa, wet):
        marks = lax.dynamic_index_in_dim(jnp.asarray(table), lax.axis_index(AXES), 0, keepdims=False)
        marks = jnp.broadcast_to(marks[:, None, None], (4 + WIN, 8, 128))
        coeff = kappa * jnp.where(wet == 1, 1.0, 0.05).astype(F32)
        packed = jnp.concatenate([load.reshape(500, 1, 128), coeff.reshape(4, 1, 128)]).reshape(504, 128)
        (packed,) = call("pack", pack_kernel, [(328, 128)], [(504, 128)], packed)
        same, other = packed if place == sorted(place) else swap(packed, to_same), swap(packed, to_other)
        part, coeff, a, b = call("unpack", unpack_kernel, [FIELD, (8, 128), (18, 8, 128), (18, 8, 128)], [], marks, same, other)
        faces = [(17, 8, 128), (17, 8, 128)]

        def trade(a, b):
            return swap(a, within), swap(b, beyond[1])

        a, b = trade(a, b)
        u, y, f, inv, a, b = call("first", first_kernel, [FIELD, FIELD, FIELD, (12, 8, 128), *faces], WORK, marks, part, coeff, a, b)

        def sweep(u, y, a, b):
            a, b = trade(a, b)
            return call("sweep", sweep_kernel, [FIELD, FIELD, *faces], WORK, marks, u, y, f, inv, coeff, a, b)

        def sweep_and_correct(u, y, a, b):
            a, b = trade(a, b)
            u, y, own, a, b = call("restrict", restrict_kernel, [FIELD, FIELD, (5, 8, 128), (22, 8, 128), (22, 8, 128)], WORK, marks, u, y, f, inv, coeff, a, b, part)
            a = swap(a, within)
            chip, near = call("chip", chip_kernel, [(10, 8, 128), (27, 8, 128)], [], marks, own, a, b)
            near, second, third = swap(near, beyond[1]), swap(chip, beyond[2]), swap(chip, beyond[3])
            (mine,) = call("side", side_kernel, [(30, 8, 128)], [], near, second, third)
            theirs = swap(mine, within)
            return call("correct", correct_kernel, [FIELD, FIELD, *faces], [FIELD, FIELD, (40, 8, 128), *WORK], marks, u, y, f, inv, coeff, a, near, chip, mine, theirs)

        u, y, a, b = sweep_and_correct(u, y, a, b)
        u, y, a, b = sweep(u, y, a, b)
        u, y, a, b = sweep(u, y, a, b)
        u, y, a, b = sweep_and_correct(u, y, a, b)
        a, b = trade(a, b)
        y, a, b, half = call("last", last_sweep_kernel, [FIELD, *faces, (328, 128)], [FIELD, *WORK], marks, u, y, f, inv, coeff, a, b)
        a, b = trade(a, b)
        half = restore(half)
        (left_half,) = call("residual", residual_kernel, [(328, 128)], [FIELD], marks, y, f, a, b)
        (solved,) = call("spread", spread_kernel, [(500, 128)], [], half)
        (rest,) = call("spread", spread_kernel, [(500, 128)], [], restore(left_half))
        return solved.reshape(load.shape), rest.reshape(load.shape)

    return run


def solution(mesh):
    sizes = tuple(mesh.shape[name] for name in AXES)
    whole = P(None, None, None, None, ("ey", "lin"), "ex")
    flat = P(None, ("ey", "lin"), "ex")
    return jax.shard_map(per_device(sizes), mesh=mesh, in_specs=(whole, flat, flat), out_specs=(whole, whole), check_vma=False)
```

```python
import math

import jax
import jax.numpy as jnp
import numpy as np
from jax import lax
from jax.experimental import pallas as pl
from jax.experimental.pallas import tpu as pltpu
from jax.sharding import PartitionSpec as P

AXES = ("ex", "ey", "lin")
N = 5
NC = 4
WIN = 14
FINE_RELAX = 0.25
COARSE_RELAX = 0.4
F32 = jnp.float32

points = np.array([-1.0, -math.sqrt(3.0 / 7.0), 0.0, math.sqrt(3.0 / 7.0), 1.0])
weights = np.array([0.1, 49.0 / 90.0, 32.0 / 45.0, 49.0 / 90.0, 0.1])


def stiffness():
    eye = np.eye(N)
    spread = points[:, None] - points[None, :] + eye
    factors = np.prod(spread, axis=1)
    deriv = factors[:, None] / (factors[None, :] * spread)
    deriv = np.where(eye > 0, (np.sum(1.0 / spread, axis=1) - 1.0)[:, None], deriv)
    return deriv.T @ (weights[:, None] * deriv)


STIFF = stiffness()
LINE = STIFF / weights[:, None]
EVEN = [[float(LINE[i, j] + LINE[i, 4 - j]) / 2 for j in range(2)] for i in range(3)]
ODD = [[float(LINE[i, j] - LINE[i, 4 - j]) / 2 for j in range(2)] for i in range(2)]
INTERP = np.stack([(1.0 - points) / 2.0, (1.0 + points) / 2.0], axis=1)
SYM = [0, 1, 2, 1, 0]


def weight(*nodes):
    return float(np.prod([weights[SYM[k]] for k in sorted(SYM[n] for n in nodes)]))


def inverse_factor(a, b, c):
    s, w = np.diag(STIFF), weights
    a, b, c = sorted(SYM[n] for n in (a, b, c))
    return FINE_RELAX / float(s[a] * w[b] * w[c] + w[a] * s[b] * w[c] + w[a] * w[b] * s[c])


def at(a, b, c):
    return a * 25 + b * 5 + c


def line(u):
    m2 = u[2] + u[2]
    e0, e1 = u[0] + u[4] - m2, u[1] + u[3] - m2
    o0, o1 = u[0] - u[4], u[1] - u[3]
    even = [EVEN[i][0] * e0 + EVEN[i][1] * e1 for i in range(3)]
    odd = [ODD[i][0] * o0 + ODD[i][1] * o1 for i in range(2)]
    return [even[0] + odd[0], even[1] + odd[1], even[2], even[1] - odd[1], even[0] - odd[0]]


class Moves:
    def __init__(self, marks=None):
        sub = lax.broadcasted_iota(jnp.int32, (8, 128), 0)
        lane = lax.broadcasted_iota(jnp.int32, (8, 128), 1)
        self.lane = lane
        self.low = sub < 4
        self.top = (sub & 3) == 3
        self.bottom = (sub & 3) == 0
        self.lane_first = lane == 0
        self.lane_last = lane == 127
        self.last = jnp.logical_and(lane == 127, sub >= 4)
        self.marks = marks
        if marks is not None:
            self.even = marks[0] > 0.5
            self.copy0 = marks[1] > 0.5

    def above(self, x):
        return jnp.where(self.top, 0.0, pltpu.roll(x, 7, 0))

    def below(self, x):
        return jnp.where(self.bottom, 0.0, pltpu.roll(x, 1, 0))

    def before(self, x):
        r = pltpu.roll(x, 1, 1)
        return jnp.where(self.lane_first, jnp.where(self.low, 0.0, pltpu.roll(r, 4, 0)), r)

    def after(self, x, end):
        r = pltpu.roll(x, 127, 1)
        return jnp.where(self.lane_last, jnp.where(self.low, pltpu.roll(r, 4, 0), end), r)

    def pick(self, x, y):
        return jnp.where(self.even, x, y)


INNER = (1, 2, 3)


def apply_operator(mv, u_ref, coeff, y_ref, acc_ref, up_ref, ready_ref=None):
    for b in range(N):
        for c in range(N):
            if ready_ref is not None and b in INNER:
                up_ref[b * 5 + c] = mv.above(u_ref[at(0, b, c)])
                continue
            u = [u_ref[at(a, b, c)] for a in range(4)]
            u.append(mv.above(u[0]))
            up_ref[b * 5 + c] = u[4]
            for a, value in enumerate(line(u)):
                acc_ref[at(a, b, c)] = value
    for a in (4, 0, 1, 2, 3):
        scale = {}
        for b in range(3):
            for c in range(b, 3):
                scale[b, c] = scale[c, b] = coeff * weight(a, b, c)
        u = [[up_ref[b * 5 + c] if a == 4 else u_ref[at(a, b, c)] for c in range(N)] for b in range(N)]
        across = [line([u[b][c] for b in range(N)]) for c in range(N)]
        for b in range(N):
            if ready_ref is not None and b in INNER:
                base = [ready_ref[at(a, b, c)] for c in range(N)]
            else:
                along = line(u[b])
                base = [acc_ref[at(a, b, c)] + along[c] for c in range(N)]
            y = [(base[c] + across[c][b]) * scale[SYM[b], SYM[c]] for c in range(N)]
            if a == 4:
                for c in range(N):
                    up_ref[b * 5 + c] = y[c]
                continue
            if a == 0:
                y = [y[c] + mv.below(up_ref[b * 5 + c]) for c in range(N)]
            y[0] = y[0] + mv.before(y[4])
            for c in range(N):
                y_ref[at(a, b, c)] = y[c]


def put_faces(mv, y_ref, a_ref, b_ref, first=0):
    ends = [jnp.zeros((8, 128), F32)] * 2
    for a in range(4):
        for c in range(4):
            low, high = y_ref[at(a, 0, c)], y_ref[at(a, 4, c)]
            a_ref[first + a * 4 + c] = mv.pick(high, low)
            b_ref[first + a * 4 + c] = mv.pick(low, high)
        for side in range(2):
            ends[side] = jnp.where(mv.lane == a, pltpu.roll(y_ref[at(a, 4 * side, 4)], a + 1, 1), ends[side])
    a_ref[first + 16] = mv.pick(ends[1], ends[0])
    b_ref[first + 16] = mv.pick(ends[0], ends[1])


def got_faces(mv, a_ref, b_ref, count, a_first=0, b_first=0):
    has_left, has_right = mv.marks[2], mv.marks[3]
    left, right = [], []
    for k in range(count):
        x, y = a_ref[a_first + k], b_ref[b_first + k]
        left.append(mv.pick(y, x) * has_left)
        right.append(mv.pick(x, y) * has_right)
    out = []
    for v in (left, right):
        rows = []
        for a in range(4):
            rows.extend(v[a * 4 : a * 4 + 4])
            rows.append(pltpu.roll(v[16], 127 - a, 1))
        out.append(rows + v[17:])
    return out


def inverse_at(inv_ref, a, b, c):
    kind = (0 if a == 0 else 6) + (0 if b == 0 else 4 if b == 4 else 2) + (0 if c == 0 else 1)
    return inv_ref[kind] * inverse_factor(a, b, c)


def residual_row(mv, f_ref, y_ref, left, right, a, b):
    row = []
    for c in range(N):
        r = f_ref[at(a, b, c)] - y_ref[at(a, b, c)]
        if b == 0:
            r = r - left[a * 5 + c]
        if b == 4:
            r = r - right[a * 5 + c]
        row.append(r)
    return row


def smooth(mv, u_ref, f_ref, y_ref, left, right, inv_ref, out_ref, mid_ref=None, rows=range(N)):
    for a in range(4):
        for b in rows:
            if mid_ref is not None and b in INNER:
                for c in range(N):
                    out_ref[at(a, b, c)] = mid_ref[at(a, b, c)]
                continue
            r = residual_row(mv, f_ref, y_ref, left, right, a, b)
            u = [u_ref[at(a, b, c)] + r[c] * inverse_at(inv_ref, a, b, c) for c in range(N)]
            u[4] = mv.after(u[0], u[4])
            for c in range(N):
                out_ref[at(a, b, c)] = u[c]


def half_rows(mv, ref, out_ref):
    def turned(x):
        return jnp.where(mv.copy0, x, pltpu.roll(x, 4, 0))

    ends = jnp.zeros((8, 128), F32)
    for k in range(20):
        for c in (0, 2):
            x, y = turned(ref[5 * k + c]), turned(ref[5 * k + c + 1])
            out_ref[pl.ds(16 * k + 4 * c, 8)] = jnp.where(mv.low, x, pltpu.roll(y, 4, 0))
        ends = jnp.where(mv.lane == k, pltpu.roll(turned(ref[5 * k + 4]), k + 1, 1), ends)
    out_ref[pl.ds(320, 8)] = ends


def pack_kernel(load_ref, out_ref, sum_ref):
    row = lax.broadcasted_iota(jnp.int32, (100, 128), 0)
    sum_ref[pl.ds(0, 100)] = load_ref[pl.ds(0, 100)] + jnp.where((row & 3) == 0, 0.0, load_ref[pl.ds(399, 100)])
    sum_ref[pl.ds(100, 404)] = load_ref[pl.ds(100, 404)]
    row = lax.broadcasted_iota(jnp.int32, (16, 128), 0)
    lane = lax.broadcasted_iota(jnp.int32, (16, 128), 1)
    moved = jnp.logical_and(row < 4, lane > 0)
    ends = jnp.zeros((16, 128), F32)
    for k in range(20):
        x = sum_ref[pl.ds(20 * k + 16, 16)]
        out_ref[pl.ds(16 * k, 16)] = sum_ref[pl.ds(20 * k, 16)] + jnp.where(moved, pltpu.roll(x, 1, 1), 0.0)
        ends = jnp.where(lane == k, pltpu.roll(x, k + 1, 1), ends)
    out_ref[pl.ds(320, 4)] = ends[:4]
    out_ref[pl.ds(324, 4)] = load_ref[pl.ds(500, 4)]


def unpack_kernel(marks, same_ref, other_ref, f_ref, coeff_ref, a_ref, b_ref):
    mv = Moves(marks)

    def pair(n):
        x, y = same_ref[pl.ds(4 * n, 8)], other_ref[pl.ds(4 * n, 8)]
        h0, h1 = jnp.where(mv.copy0, x, y), jnp.where(mv.copy0, y, x)
        return jnp.where(mv.low, h0, pltpu.roll(h1, 4, 0)), jnp.where(mv.low, pltpu.roll(h0, 4, 0), h1)

    ends, coeff = pair(80)
    coeff_ref[...] = coeff
    joint = jnp.logical_and(mv.lane_first, jnp.logical_not(mv.low))
    for k in range(20):
        for c in (0, 2):
            f_ref[5 * k + c], f_ref[5 * k + c + 1] = pair(4 * k + c)
        over = pltpu.roll(pltpu.roll(ends, (128 - k) % 128, 1), 4, 0)
        f_ref[5 * k] = f_ref[5 * k] + jnp.where(joint, over, 0.0)
        f_ref[5 * k + 4] = pltpu.roll(ends, 127 - k, 1)
    put_faces(mv, f_ref, a_ref, b_ref)
    a_ref[17] = coeff
    b_ref[17] = coeff


def first_kernel(marks, part_ref, coeff_ref, ga_ref, gb_ref, u_ref, y_ref, f_ref, inv_ref, a_ref, b_ref, acc_ref, up_ref):
    mv = Moves(marks)
    left, right = got_faces(mv, ga_ref, gb_ref, 18)
    coeff = coeff_ref[...]
    for kind_b, value in enumerate((coeff + left[20], coeff, coeff + right[20])):
        for kind_a, v in enumerate((value + mv.below(value), value)):
            inv_ref[kind_a * 6 + kind_b * 2] = 1.0 / (v + mv.before(v))
            inv_ref[kind_a * 6 + kind_b * 2 + 1] = 1.0 / v
    for a in range(4):
        for b in range(N):
            f = [part_ref[at(a, b, c)] for c in range(N)]
            if b == 0:
                f = [f[c] + left[a * 5 + c] for c in range(N)]
            if b == 4:
                f = [f[c] + right[a * 5 + c] for c in range(N)]
            u = [f[c] * inverse_at(inv_ref, a, b, c) for c in range(N)]
            u[4] = mv.after(u[0], u[4])
            for c in range(N):
                f_ref[at(a, b, c)] = f[c]
                u_ref[at(a, b, c)] = u[c]
    apply_operator(mv, u_ref, coeff, y_ref, acc_ref, up_ref)
    put_faces(mv, y_ref, a_ref, b_ref)


def inner_kernel(u_ref, y_ref, f_ref, inv_ref, mid_ref, ready_ref):
    mv = Moves()
    smooth(mv, u_ref, f_ref, y_ref, None, None, inv_ref, mid_ref, None, INNER)
    for b in INNER:
        planes = []
        for c in range(N):
            u = [mid_ref[at(a, b, c)] for a in range(4)]
            u.append(mv.above(u[0]))
            planes.append(u[4])
            for a, value in enumerate(line(u)):
                ready_ref[at(a, b, c)] = value
        for a in range(N):
            for c, value in enumerate(line(planes if a == 4 else [mid_ref[at(a, b, c)] for c in range(N)])):
                ready_ref[at(a, b, c)] = ready_ref[at(a, b, c)] + value


def sweep_kernel(marks, u_ref, y_ref, f_ref, inv_ref, coeff_ref, mid_ref, ready_ref, ga_ref, gb_ref, un_ref, yn_ref, a_ref, b_ref, acc_ref, up_ref):
    mv = Moves(marks)
    left, right = got_faces(mv, ga_ref, gb_ref, 17)
    smooth(mv, u_ref, f_ref, y_ref, left, right, inv_ref, un_ref, mid_ref)
    apply_operator(mv, un_ref, coeff_ref[...], yn_ref, acc_ref, up_ref, ready_ref)
    put_faces(mv, yn_ref, a_ref, b_ref)


def last_sweep_kernel(marks, u_ref, y_ref, f_ref, inv_ref, coeff_ref, mid_ref, ready_ref, ga_ref, gb_ref, yn_ref, a_ref, b_ref, half_ref, un_ref, acc_ref, up_ref):
    sweep_kernel(marks, u_ref, y_ref, f_ref, inv_ref, coeff_ref, mid_ref, ready_ref, ga_ref, gb_ref, un_ref, yn_ref, a_ref, b_ref, acc_ref, up_ref)
    half_rows(Moves(marks), un_ref, half_ref)


def restrict_kernel(marks, u_ref, y_ref, f_ref, inv_ref, coeff_ref, mid_ref, ready_ref, ga_ref, gb_ref, part_ref, un_ref, yn_ref, own_ref, a_ref, b_ref, acc_ref, up_ref):
    mv = Moves(marks)
    left, right = got_faces(mv, ga_ref, gb_ref, 17)
    smooth(mv, u_ref, f_ref, y_ref, left, right, inv_ref, un_ref, mid_ref)
    apply_operator(mv, un_ref, coeff_ref[...], yn_ref, acc_ref, up_ref, ready_ref)
    put_faces(mv, yn_ref, a_ref, b_ref, 5)
    z = [[], []]
    for c in range(N):
        rows = [[], []]
        for a in range(4):
            r = [part_ref[at(a, b, c)] - yn_ref[at(a, b, c)] for b in range(N)]
            inner = [sum(float(INTERP[b, side]) * r[b] for b in (1, 2, 3)) for side in range(2)]
            rows[0].append(r[0] + inner[0])
            rows[1].append(r[4] + inner[1])
        for side in range(2):
            x = rows[side]
            low = x[0] + sum(float(INTERP[a, 0]) * x[a] for a in (1, 2, 3))
            z[side].append(low + mv.below(sum(float(INTERP[a, 1]) * x[a] for a in (1, 2, 3))))
    for side in range(2):
        x = z[side]
        inner = [sum(float(INTERP[c, k]) * x[c] for c in (1, 2, 3)) for k in range(2)]
        own_ref[side * 2] = x[0] + inner[0] + mv.before(inner[1])
        own_ref[side * 2 + 1] = jnp.where(mv.last, x[4] + inner[1], 0.0)
    own_ref[4] = coeff_ref[...]
    for k in range(5):
        a_ref[k] = own_ref[k]


def chip_kernel(marks, own_ref, ga_ref, b_ref, chip_ref, near_ref):
    mv = Moves(marks)
    for k in range(5):
        x, y = own_ref[k], ga_ref[k]
        low, high = mv.pick(x, y), mv.pick(y, x)
        chip_ref[k] = low
        chip_ref[5 + k] = high
        near_ref[k] = low
        near_ref[5 + k] = high
    for k in range(17):
        near_ref[10 + k] = b_ref[5 + k]


def side_kernel(near_ref, second_ref, third_ref, out_ref):
    for k in range(10):
        out_ref[k] = near_ref[k]
        out_ref[10 + k] = second_ref[k]
        out_ref[20 + k] = third_ref[k]


def coarse_solve(mv, chip_ref, mine_ref, other_ref):
    window = []
    for w in range(WIN):
        rows = []
        ok = mv.marks[4 + w]
        for k in range(5):
            if w in (6, 7):
                rows.append(chip_ref[(w - 6) * 5 + k])
                continue
            if w < 6:
                slot = (2 - w // 2) * 10 + (w % 2) * 5 + k
                x = mv.pick(mine_ref[slot], other_ref[slot])
            else:
                slot = (w // 2 - 4) * 10 + (w % 2) * 5 + k
                x = mv.pick(other_ref[slot], mine_ref[slot])
            rows.append(x * ok)
        window.append(rows)
    coeffs = [rows[4] for rows in window]
    load, inverse, value = {}, {}, {}
    factor = COARSE_RELAX / (2.0 / 3.0)
    for j in range(2, 13):
        load[j] = [window[j - 1][2 + g] + window[j][g] for g in range(2)]
        k = coeffs[j - 1] + coeffs[j]
        k = k + mv.below(k)
        inverse[j] = [jnp.where(v > 0.0, factor / v, 0.0) for v in (k + mv.before(k), k)]
        value[j] = [inverse[j][g] * load[j][g] for g in range(2)]
    for step in range(NC - 1):
        first, final = 2 + step, 12 - step
        nodes = {}
        for j in range(first, final + 1):
            value[j][1] = mv.after(value[j][0], value[j][1])
            nodes[j] = [value[j], [mv.above(v) for v in value[j]]]
        sums = {j: [[None, None], [None, None]] for j in range(first, final + 1)}
        for j in range(first, final):
            v = {(a, b, c): nodes[j + b][a][c] for a in range(2) for b in range(2) for c in range(2)}
            for axis in range(3):
                v = butterfly(v, axis)
            cf = [coeffs[j] * 0.125, coeffs[j] * (0.125 * 2.0 / 3.0), coeffs[j] * (0.125 / 3.0)]
            v = {key: None if sum(key) == 0 else x * cf[sum(key) - 1] for key, x in v.items()}
            for axis in range(3):
                v = butterfly(v, axis)
            for (a, b, c), x in v.items():
                old = sums[j + b][a][c]
                sums[j + b][a][c] = x if old is None else old + x
        new = {}
        for j in range(first + 1, final):
            s = sums[j]
            row = [s[0][c] + mv.below(s[1][c]) for c in range(2)]
            row[0] = row[0] + mv.before(row[1])
            new[j] = [value[j][g] + inverse[j][g] * (load[j][g] - row[g]) for g in range(2)]
        value = new
    for j in value:
        value[j][1] = mv.after(value[j][0], value[j][1])
    lines = [[mv.pick(value[5 + m][g], value[6 + m][g]) for g in range(2)] for m in range(4)]
    return lines, mv.pick(coeffs[5], coeffs[6]), mv.pick(coeffs[7], coeffs[8])


def butterfly(v, axis):
    out = {}
    for key in v:
        if key[axis]:
            continue
        up = tuple(1 if k == axis else key[k] for k in range(3))
        x, y = v[key], v[up]
        out[key] = y if x is None else x + y
        out[up] = -y if x is None else x - y
    return out


def nodal(mv, pair, count):
    rows = []
    up = [mv.above(v) for v in pair]
    for a in range(count):
        lo, hi = float(INTERP[a, 0]), float(INTERP[a, 1])
        if a == 0:
            ends = pair
        elif a == 4:
            ends = up
        else:
            ends = [lo * pair[g] + hi * up[g] for g in range(2)]
        rows.append([ends[0] if c == 0 else ends[1] if c == 4 else float(INTERP[c, 0]) * ends[0] + float(INTERP[c, 1]) * ends[1] for c in range(N)])
    return rows


def neighbour_face(mv, near, far, coeff):
    w = [float(x) for x in weights]
    x = nodal(mv, near, N)
    z = nodal(mv, far, N)
    y = []
    for a in range(N):
        row = []
        for c in range(N):
            v = (x[a][c] - z[a][c]) * (0.5 * weight(a, c))
            if a in (0, 4):
                v = v + (x[a][c] - x[4 - a][c]) * (0.5 * w[0] * w[SYM[c]])
            if c in (0, 4):
                v = v + (x[a][c] - x[a][4 - c]) * (0.5 * w[0] * w[SYM[a]])
            row.append(v * coeff)
        y.append(row)
    out = []
    for a in range(4):
        row = [y[0][c] + mv.below(y[4][c]) for c in range(N)] if a == 0 else y[a]
        row[0] = row[0] + mv.before(row[4])
        out.extend(row)
    return out


def add_correction(mv, low, high, coeff, u_ref, y_ref, ua_ref, ya_ref):
    half = coeff * 0.5
    found = {}

    def v(a, b, c):
        if (a, b, c) not in found:
            lo, hi = low[a][c], high[a][c]
            found[a, b, c] = lo if b == 0 else hi if b == 4 else float(INTERP[b, 0]) * lo + float(INTERP[b, 1]) * hi
        return found[a, b, c]

    def share(a, b, c):
        parts = []
        if a in (0, 4):
            parts.append((v(a, b, c) - v(4 - a, b, c)) * weight(b, c))
        if b in (0, 4):
            parts.append((v(a, b, c) - v(a, 4 - b, c)) * weight(a, c))
        if c in (0, 4):
            parts.append((v(a, b, c) - v(a, b, 4 - c)) * weight(a, b))
        return sum(parts[1:], parts[0]) * half if parts else None

    for a in range(4):
        for b in range(N):
            row = [share(a, b, c) for c in range(N)]
            if a == 0:
                for c in range(N):
                    under = share(4, b, c)
                    row[c] = row[c] + mv.below(under)
            row[0] = row[0] + mv.before(row[4])
            for c in range(N):
                ua_ref[at(a, b, c)] = u_ref[at(a, b, c)] + v(a, b, c)
                ya_ref[at(a, b, c)] = y_ref[at(a, b, c)] if row[c] is None else y_ref[at(a, b, c)] + row[c]


def correct_kernel(marks, u_ref, y_ref, f_ref, inv_ref, coeff_ref, ga_ref, near_ref, chip_ref, mine_ref, other_ref, un_ref, yn_ref, a_ref, b_ref, ua_ref, ya_ref, face_ref, acc_ref, up_ref):
    mv = Moves(marks)
    coeff = coeff_ref[...]
    lines, coeff_left, coeff_right = coarse_solve(mv, chip_ref, mine_ref, other_ref)
    for k, v in enumerate(neighbour_face(mv, lines[1], lines[0], coeff_left)):
        face_ref[k] = v
    for k, v in enumerate(neighbour_face(mv, lines[2], lines[3], coeff_right)):
        face_ref[20 + k] = v
    low, high = nodal(mv, lines[1], N), nodal(mv, lines[2], N)
    add_correction(mv, low, high, coeff, u_ref, y_ref, ua_ref, ya_ref)
    left, right = got_faces(mv, ga_ref, near_ref, 17, 5, 10)
    left = [left[k] + face_ref[k] for k in range(20)]
    right = [right[k] + face_ref[20 + k] for k in range(20)]
    smooth(mv, ua_ref, f_ref, ya_ref, left, right, inv_ref, un_ref)
    apply_operator(mv, un_ref, coeff, yn_ref, acc_ref, up_ref)
    put_faces(mv, yn_ref, a_ref, b_ref)


def residual_kernel(marks, y_ref, f_ref, ga_ref, gb_ref, half_ref, r_ref):
    mv = Moves(marks)
    left, right = got_faces(mv, ga_ref, gb_ref, 17)
    for a in range(4):
        for b in range(N):
            r = residual_row(mv, f_ref, y_ref, left, right, a, b)
            r[4] = mv.after(r[0], r[4])
            for c in range(N):
                r_ref[at(a, b, c)] = r[c]
    half_rows(mv, r_ref, half_ref)


def spread_kernel(half_ref, out_ref):
    lane = lax.broadcasted_iota(jnp.int32, (8, 128), 1)
    ends = half_ref[pl.ds(320, 8)]
    for k in range(20):
        out_ref[pl.ds(20 * k, 16)] = half_ref[pl.ds(16 * k, 16)]
        last = jnp.where(lane == 127, pltpu.roll(ends, 127 - k, 1), pltpu.roll(half_ref[pl.ds(16 * k, 8)], 127, 1))
        out_ref[pl.ds(20 * k + 16, 4)] = last[:4]
    row = lax.broadcasted_iota(jnp.int32, (100, 128), 0)
    out_ref[pl.ds(400, 100)] = jnp.where((row & 3) == 3, 0.0, out_ref[pl.ds(1, 100)])


VM = pl.BlockSpec(memory_space=pltpu.VMEM)
FIELD = (100, 8, 128)
WORK = [(125, 8, 128), (25, 8, 128)]


def call(name, kernel, outs, scratch, *args, cost=None):
    return pl.pallas_call(
        kernel,
        out_shape=[jax.ShapeDtypeStruct(s, F32) for s in outs],
        in_specs=[VM] * len(args),
        out_specs=[VM] * len(outs),
        scratch_shapes=[pltpu.VMEM(s, F32) for s in scratch],
        compiler_params=pltpu.CompilerParams(vmem_limit_bytes=12 * 1024 * 1024),
        name=name,
        cost_estimate=cost,
    )(*args)


def placement(sizes):
    _, ey, lin = sizes
    place = list(range(ey * lin))
    if lin == 64:
        for s in place[:]:
            side, p, y, core = s // 64, s // 8 % 8, s // 2 % 4, s % 2
            z = (p - side) % 8
            place[s] = side * 64 + z * 8 + (3 - y if p % 2 else y) * 2 + core
    return place


def per_device(sizes):
    strips = sizes[1] * sizes[2]
    chips = strips // 2
    place = placement(sizes)
    device = [[copy * strips + place[s] for s in range(strips)] for copy in range(2)]
    to_same = [(e * strips + s, device[e][s]) for e in range(2) for s in range(strips)]
    to_other = [(e * strips + s, device[1 - e][s]) for e in range(2) for s in range(strips)]
    back = [(b, a) for a, b in to_same]
    within = [(device[e][s], device[e][s ^ 1]) for e in range(2) for s in range(strips)]

    def chip_pairs(d):
        pairs = []
        for e in range(2):
            for s in range(strips):
                k = s // 2 - d if s % 2 == 0 else s // 2 + d
                if 0 <= k < chips:
                    pairs.append((device[e][s], device[e][2 * k + 1 - s % 2]))
                else:
                    pairs.append((device[e][s], device[1 - e][s]))
        return pairs

    beyond = {d: chip_pairs(d) for d in (1, 2, 3)}
    table = np.zeros((2 * strips, 4 + WIN), np.float32)
    for copy in range(2):
        for s in range(strips):
            window = [0 <= s - s % 2 - 6 + w < strips for w in range(WIN)]
            table[device[copy][s]] = [s % 2 == 0, copy == 0, s > 0, s < strips - 1, *window]

    def swap(x, pairs):
        return lax.ppermute(x, AXES, pairs)

    def restore(x):
        return x if place == sorted(place) else swap(x, back)

    def run(load, kappa, wet):
        marks = lax.dynamic_index_in_dim(jnp.asarray(table), lax.axis_index(AXES), 0, keepdims=False)
        marks = jnp.broadcast_to(marks[:, None, None], (4 + WIN, 8, 128))
        coeff = kappa * jnp.where(wet == 1, 1.0, 0.05).astype(F32)
        packed = jnp.concatenate([load.reshape(500, 1, 128), coeff.reshape(4, 1, 128)]).reshape(504, 128)
        (packed,) = call("pack", pack_kernel, [(328, 128)], [(504, 128)], packed)
        same, other = packed if place == sorted(place) else swap(packed, to_same), swap(packed, to_other)
        part, coeff, a, b = call("unpack", unpack_kernel, [FIELD, (8, 128), (18, 8, 128), (18, 8, 128)], [], marks, same, other)
        faces = [(17, 8, 128), (17, 8, 128)]

        def trade(a, b):
            return swap(a, within), swap(b, beyond[1])

        a, b = trade(a, b)
        u, y, f, inv, a, b = call("first", first_kernel, [FIELD, FIELD, FIELD, (12, 8, 128), *faces], WORK, marks, part, coeff, a, b)

        def inner(u, y):
            cost = pl.CostEstimate(flops=2000000, bytes_accessed=1500000, transcendentals=0)
            return call("inner", inner_kernel, [FIELD, (125, 8, 128)], [], u, y, f, inv, cost=cost)

        def sweep(u, y, a, b):
            a, b = trade(a, b)
            return call("sweep", sweep_kernel, [FIELD, FIELD, *faces], WORK, marks, u, y, f, inv, coeff, *inner(u, y), a, b)

        def sweep_and_correct(u, y, a, b):
            a, b = trade(a, b)
            u, y, own, a, b = call("restrict", restrict_kernel, [FIELD, FIELD, (5, 8, 128), (22, 8, 128), (22, 8, 128)], WORK, marks, u, y, f, inv, coeff, *inner(u, y), a, b, part)
            a = swap(a, within)
            chip, near = call("chip", chip_kernel, [(10, 8, 128), (27, 8, 128)], [], marks, own, a, b)
            near, second, third = swap(near, beyond[1]), swap(chip, beyond[2]), swap(chip, beyond[3])
            (mine,) = call("side", side_kernel, [(30, 8, 128)], [], near, second, third)
            theirs = swap(mine, within)
            return call("correct", correct_kernel, [FIELD, FIELD, *faces], [FIELD, FIELD, (40, 8, 128), *WORK], marks, u, y, f, inv, coeff, a, near, chip, mine, theirs)

        u, y, a, b = sweep_and_correct(u, y, a, b)
        u, y, a, b = sweep(u, y, a, b)
        u, y, a, b = sweep(u, y, a, b)
        u, y, a, b = sweep_and_correct(u, y, a, b)
        a, b = trade(a, b)
        y, a, b, half = call("last", last_sweep_kernel, [FIELD, *faces, (328, 128)], [FIELD, *WORK], marks, u, y, f, inv, coeff, *inner(u, y), a, b)
        a, b = trade(a, b)
        half = restore(half)
        (left_half,) = call("residual", residual_kernel, [(328, 128)], [FIELD], marks, y, f, a, b)
        (solved,) = call("spread", spread_kernel, [(500, 128)], [], half)
        (rest,) = call("spread", spread_kernel, [(500, 128)], [], restore(left_half))
        return solved.reshape(load.shape), rest.reshape(load.shape)

    return run


def solution(mesh):
    sizes = tuple(mesh.shape[name] for name in AXES)
    whole = P(None, None, None, None, ("ey", "lin"), "ex")
    flat = P(None, ("ey", "lin"), "ex")
    return jax.shard_map(per_device(sizes), mesh=mesh, in_specs=(whole, flat, flat), out_specs=(whole, whole), check_vma=False)
```

```python
import math

import jax
import jax.numpy as jnp
import numpy as np
from jax import lax
from jax.experimental import pallas as pl
from jax.experimental.pallas import tpu as pltpu
from jax.sharding import PartitionSpec as P

AXES = ("ex", "ey", "lin")
N = 5
NC = 4
WIN = 14
FINE_RELAX = 0.25
COARSE_RELAX = 0.4
F32 = jnp.float32

points = np.array([-1.0, -math.sqrt(3.0 / 7.0), 0.0, math.sqrt(3.0 / 7.0), 1.0])
weights = np.array([0.1, 49.0 / 90.0, 32.0 / 45.0, 49.0 / 90.0, 0.1])


def stiffness():
    eye = np.eye(N)
    spread = points[:, None] - points[None, :] + eye
    factors = np.prod(spread, axis=1)
    deriv = factors[:, None] / (factors[None, :] * spread)
    deriv = np.where(eye > 0, (np.sum(1.0 / spread, axis=1) - 1.0)[:, None], deriv)
    return deriv.T @ (weights[:, None] * deriv)


STIFF = stiffness()
LINE = STIFF / weights[:, None]
EVEN = [[float(LINE[i, j] + LINE[i, 4 - j]) / 2 for j in range(2)] for i in range(3)]
ODD = [[float(LINE[i, j] - LINE[i, 4 - j]) / 2 for j in range(2)] for i in range(2)]
INTERP = np.stack([(1.0 - points) / 2.0, (1.0 + points) / 2.0], axis=1)
SYM = [0, 1, 2, 1, 0]


def weight(*nodes):
    return float(np.prod([weights[SYM[k]] for k in sorted(SYM[n] for n in nodes)]))


def inverse_factor(a, b, c):
    s, w = np.diag(STIFF), weights
    a, b, c = sorted(SYM[n] for n in (a, b, c))
    return FINE_RELAX / float(s[a] * w[b] * w[c] + w[a] * s[b] * w[c] + w[a] * w[b] * s[c])


def at(a, b, c):
    return a * 25 + b * 5 + c


def line(u):
    m2 = u[2] + u[2]
    e0, e1 = u[0] + u[4] - m2, u[1] + u[3] - m2
    o0, o1 = u[0] - u[4], u[1] - u[3]
    even = [EVEN[i][0] * e0 + EVEN[i][1] * e1 for i in range(3)]
    odd = [ODD[i][0] * o0 + ODD[i][1] * o1 for i in range(2)]
    return [even[0] + odd[0], even[1] + odd[1], even[2], even[1] - odd[1], even[0] - odd[0]]


class Moves:
    def __init__(self, marks=None):
        sub = lax.broadcasted_iota(jnp.int32, (8, 128), 0)
        lane = lax.broadcasted_iota(jnp.int32, (8, 128), 1)
        self.lane = lane
        self.low = sub < 4
        self.top = (sub & 3) == 3
        self.bottom = (sub & 3) == 0
        self.lane_first = lane == 0
        self.lane_last = lane == 127
        self.last = jnp.logical_and(lane == 127, sub >= 4)
        self.marks = marks
        if marks is not None:
            self.even = marks[0] > 0.5
            self.copy0 = marks[1] > 0.5

    def above(self, x):
        return jnp.where(self.top, 0.0, pltpu.roll(x, 7, 0))

    def below(self, x):
        return jnp.where(self.bottom, 0.0, pltpu.roll(x, 1, 0))

    def before(self, x):
        r = pltpu.roll(x, 1, 1)
        return jnp.where(self.lane_first, jnp.where(self.low, 0.0, pltpu.roll(r, 4, 0)), r)

    def after(self, x, end):
        r = pltpu.roll(x, 127, 1)
        return jnp.where(self.lane_last, jnp.where(self.low, pltpu.roll(r, 4, 0), end), r)

    def pick(self, x, y):
        return jnp.where(self.even, x, y)


INNER = (1, 2, 3)


def apply_operator(mv, u_ref, coeff, y_ref, acc_ref, up_ref, ready_ref=None):
    for b in range(N):
        for c in range(N):
            if ready_ref is not None and b in INNER:
                up_ref[b * 5 + c] = mv.above(u_ref[at(0, b, c)])
                continue
            u = [u_ref[at(a, b, c)] for a in range(4)]
            u.append(mv.above(u[0]))
            up_ref[b * 5 + c] = u[4]
            for a, value in enumerate(line(u)):
                acc_ref[at(a, b, c)] = value
    for a in (4, 0, 1, 2, 3):
        scale = {}
        for b in range(3):
            for c in range(b, 3):
                scale[b, c] = scale[c, b] = coeff * weight(a, b, c)
        u = [[up_ref[b * 5 + c] if a == 4 else u_ref[at(a, b, c)] for c in range(N)] for b in range(N)]
        across = [line([u[b][c] for b in range(N)]) for c in range(N)]
        for b in range(N):
            if ready_ref is not None and b in INNER:
                base = [ready_ref[at(a, b, c)] for c in range(N)]
            else:
                along = line(u[b])
                base = [acc_ref[at(a, b, c)] + along[c] for c in range(N)]
            y = [(base[c] + across[c][b]) * scale[SYM[b], SYM[c]] for c in range(N)]
            if a == 4:
                for c in range(N):
                    up_ref[b * 5 + c] = y[c]
                continue
            if a == 0:
                y = [y[c] + mv.below(up_ref[b * 5 + c]) for c in range(N)]
            y[0] = y[0] + mv.before(y[4])
            for c in range(N):
                y_ref[at(a, b, c)] = y[c]


def put_faces(mv, y_ref, a_ref, b_ref, first=0):
    ends = [jnp.zeros((8, 128), F32)] * 2
    for a in range(4):
        for c in range(4):
            low, high = y_ref[at(a, 0, c)], y_ref[at(a, 4, c)]
            a_ref[first + a * 4 + c] = mv.pick(high, low)
            b_ref[first + a * 4 + c] = mv.pick(low, high)
        for side in range(2):
            ends[side] = jnp.where(mv.lane == a, pltpu.roll(y_ref[at(a, 4 * side, 4)], a + 1, 1), ends[side])
    a_ref[first + 16] = mv.pick(ends[1], ends[0])
    b_ref[first + 16] = mv.pick(ends[0], ends[1])


def got_faces(mv, a_ref, b_ref, count, a_first=0, b_first=0):
    has_left, has_right = mv.marks[2], mv.marks[3]
    left, right = [], []
    for k in range(count):
        x, y = a_ref[a_first + k], b_ref[b_first + k]
        left.append(mv.pick(y, x) * has_left)
        right.append(mv.pick(x, y) * has_right)
    out = []
    for v in (left, right):
        rows = []
        for a in range(4):
            rows.extend(v[a * 4 : a * 4 + 4])
            rows.append(pltpu.roll(v[16], 127 - a, 1))
        out.append(rows + v[17:])
    return out


def inverse_at(inv_ref, a, b, c):
    kind = (0 if a == 0 else 6) + (0 if b == 0 else 4 if b == 4 else 2) + (0 if c == 0 else 1)
    return inv_ref[kind] * inverse_factor(a, b, c)


def residual_row(mv, f_ref, y_ref, left, right, a, b):
    row = []
    for c in range(N):
        r = f_ref[at(a, b, c)] - y_ref[at(a, b, c)]
        if b == 0:
            r = r - left[a * 5 + c]
        if b == 4:
            r = r - right[a * 5 + c]
        row.append(r)
    return row


def smooth(mv, u_ref, f_ref, y_ref, left, right, inv_ref, out_ref, mid_ref=None, rows=range(N)):
    for a in range(4):
        for b in rows:
            if mid_ref is not None and b in INNER:
                for c in range(N):
                    out_ref[at(a, b, c)] = mid_ref[at(a, b, c)]
                continue
            r = residual_row(mv, f_ref, y_ref, left, right, a, b)
            u = [u_ref[at(a, b, c)] + r[c] * inverse_at(inv_ref, a, b, c) for c in range(N)]
            u[4] = mv.after(u[0], u[4])
            for c in range(N):
                out_ref[at(a, b, c)] = u[c]


def half_rows(mv, ref, out_ref):
    def turned(x):
        return jnp.where(mv.copy0, x, pltpu.roll(x, 4, 0))

    ends = jnp.zeros((8, 128), F32)
    for k in range(20):
        for c in (0, 2):
            x, y = turned(ref[5 * k + c]), turned(ref[5 * k + c + 1])
            out_ref[pl.ds(16 * k + 4 * c, 8)] = jnp.where(mv.low, x, pltpu.roll(y, 4, 0))
        ends = jnp.where(mv.lane == k, pltpu.roll(turned(ref[5 * k + 4]), k + 1, 1), ends)
    out_ref[pl.ds(320, 8)] = ends


def pack_kernel(load_ref, out_ref, sum_ref):
    row = lax.broadcasted_iota(jnp.int32, (100, 128), 0)
    sum_ref[pl.ds(0, 100)] = load_ref[pl.ds(0, 100)] + jnp.where((row & 3) == 0, 0.0, load_ref[pl.ds(399, 100)])
    sum_ref[pl.ds(100, 404)] = load_ref[pl.ds(100, 404)]
    row = lax.broadcasted_iota(jnp.int32, (16, 128), 0)
    lane = lax.broadcasted_iota(jnp.int32, (16, 128), 1)
    moved = jnp.logical_and(row < 4, lane > 0)
    ends = jnp.zeros((16, 128), F32)
    for k in range(20):
        x = sum_ref[pl.ds(20 * k + 16, 16)]
        out_ref[pl.ds(16 * k, 16)] = sum_ref[pl.ds(20 * k, 16)] + jnp.where(moved, pltpu.roll(x, 1, 1), 0.0)
        ends = jnp.where(lane == k, pltpu.roll(x, k + 1, 1), ends)
    out_ref[pl.ds(320, 4)] = ends[:4]
    out_ref[pl.ds(324, 4)] = load_ref[pl.ds(500, 4)]


def unpack_kernel(marks, same_ref, other_ref, f_ref, coeff_ref, a_ref, b_ref):
    mv = Moves(marks)

    def pair(n):
        x, y = same_ref[pl.ds(4 * n, 8)], other_ref[pl.ds(4 * n, 8)]
        h0, h1 = jnp.where(mv.copy0, x, y), jnp.where(mv.copy0, y, x)
        return jnp.where(mv.low, h0, pltpu.roll(h1, 4, 0)), jnp.where(mv.low, pltpu.roll(h0, 4, 0), h1)

    ends, coeff = pair(80)
    coeff_ref[...] = coeff
    joint = jnp.logical_and(mv.lane_first, jnp.logical_not(mv.low))
    for k in range(20):
        for c in (0, 2):
            f_ref[5 * k + c], f_ref[5 * k + c + 1] = pair(4 * k + c)
        over = pltpu.roll(pltpu.roll(ends, (128 - k) % 128, 1), 4, 0)
        f_ref[5 * k] = f_ref[5 * k] + jnp.where(joint, over, 0.0)
        f_ref[5 * k + 4] = pltpu.roll(ends, 127 - k, 1)
    put_faces(mv, f_ref, a_ref, b_ref)
    a_ref[17] = coeff
    b_ref[17] = coeff


def first_kernel(marks, part_ref, coeff_ref, ga_ref, gb_ref, u_ref, y_ref, f_ref, inv_ref, a_ref, b_ref, acc_ref, up_ref):
    mv = Moves(marks)
    left, right = got_faces(mv, ga_ref, gb_ref, 18)
    coeff = coeff_ref[...]
    for kind_b, value in enumerate((coeff + left[20], coeff, coeff + right[20])):
        for kind_a, v in enumerate((value + mv.below(value), value)):
            inv_ref[kind_a * 6 + kind_b * 2] = 1.0 / (v + mv.before(v))
            inv_ref[kind_a * 6 + kind_b * 2 + 1] = 1.0 / v
    for a in range(4):
        for b in range(N):
            f = [part_ref[at(a, b, c)] for c in range(N)]
            if b == 0:
                f = [f[c] + left[a * 5 + c] for c in range(N)]
            if b == 4:
                f = [f[c] + right[a * 5 + c] for c in range(N)]
            u = [f[c] * inverse_at(inv_ref, a, b, c) for c in range(N)]
            u[4] = mv.after(u[0], u[4])
            for c in range(N):
                f_ref[at(a, b, c)] = f[c]
                u_ref[at(a, b, c)] = u[c]
    apply_operator(mv, u_ref, coeff, y_ref, acc_ref, up_ref)
    put_faces(mv, y_ref, a_ref, b_ref)


def inner_kernel(u_ref, y_ref, f_ref, inv_ref, mid_ref, ready_ref):
    mv = Moves()
    smooth(mv, u_ref, f_ref, y_ref, None, None, inv_ref, mid_ref, None, INNER)
    for b in INNER:
        planes = []
        for c in range(N):
            u = [mid_ref[at(a, b, c)] for a in range(4)]
            u.append(mv.above(u[0]))
            planes.append(u[4])
            for a, value in enumerate(line(u)):
                ready_ref[at(a, b, c)] = value
        for a in range(N):
            for c, value in enumerate(line(planes if a == 4 else [mid_ref[at(a, b, c)] for c in range(N)])):
                ready_ref[at(a, b, c)] = ready_ref[at(a, b, c)] + value


def sweep_kernel(marks, u_ref, y_ref, f_ref, inv_ref, coeff_ref, mid_ref, ready_ref, ga_ref, gb_ref, un_ref, yn_ref, a_ref, b_ref, acc_ref, up_ref):
    mv = Moves(marks)
    left, right = got_faces(mv, ga_ref, gb_ref, 17)
    smooth(mv, u_ref, f_ref, y_ref, left, right, inv_ref, un_ref, mid_ref)
    apply_operator(mv, un_ref, coeff_ref[...], yn_ref, acc_ref, up_ref, ready_ref)
    put_faces(mv, yn_ref, a_ref, b_ref)


def last_sweep_kernel(marks, u_ref, y_ref, f_ref, inv_ref, coeff_ref, mid_ref, ready_ref, ga_ref, gb_ref, yn_ref, a_ref, b_ref, half_ref, un_ref, acc_ref, up_ref):
    sweep_kernel(marks, u_ref, y_ref, f_ref, inv_ref, coeff_ref, mid_ref, ready_ref, ga_ref, gb_ref, un_ref, yn_ref, a_ref, b_ref, acc_ref, up_ref)
    half_rows(Moves(marks), un_ref, half_ref)


def restrict_kernel(marks, u_ref, y_ref, f_ref, inv_ref, coeff_ref, mid_ref, ready_ref, ga_ref, gb_ref, part_ref, un_ref, yn_ref, own_ref, a_ref, b_ref, acc_ref, up_ref):
    mv = Moves(marks)
    left, right = got_faces(mv, ga_ref, gb_ref, 17)
    smooth(mv, u_ref, f_ref, y_ref, left, right, inv_ref, un_ref, mid_ref)
    apply_operator(mv, un_ref, coeff_ref[...], yn_ref, acc_ref, up_ref, ready_ref)
    put_faces(mv, yn_ref, a_ref, b_ref, 5)
    z = [[], []]
    for c in range(N):
        rows = [[], []]
        for a in range(4):
            r = [part_ref[at(a, b, c)] - yn_ref[at(a, b, c)] for b in range(N)]
            inner = [sum(float(INTERP[b, side]) * r[b] for b in (1, 2, 3)) for side in range(2)]
            rows[0].append(r[0] + inner[0])
            rows[1].append(r[4] + inner[1])
        for side in range(2):
            x = rows[side]
            low = x[0] + sum(float(INTERP[a, 0]) * x[a] for a in (1, 2, 3))
            z[side].append(low + mv.below(sum(float(INTERP[a, 1]) * x[a] for a in (1, 2, 3))))
    for side in range(2):
        x = z[side]
        inner = [sum(float(INTERP[c, k]) * x[c] for c in (1, 2, 3)) for k in range(2)]
        own_ref[side * 2] = x[0] + inner[0] + mv.before(inner[1])
        own_ref[side * 2 + 1] = jnp.where(mv.last, x[4] + inner[1], 0.0)
    own_ref[4] = coeff_ref[...]
    for k in range(5):
        a_ref[k] = own_ref[k]


def chip_kernel(marks, own_ref, ga_ref, b_ref, chip_ref, near_ref):
    mv = Moves(marks)
    for k in range(5):
        x, y = own_ref[k], ga_ref[k]
        low, high = mv.pick(x, y), mv.pick(y, x)
        chip_ref[k] = low
        chip_ref[5 + k] = high
        near_ref[k] = low
        near_ref[5 + k] = high
    for k in range(17):
        near_ref[10 + k] = b_ref[5 + k]


def side_kernel(near_ref, second_ref, third_ref, out_ref):
    for k in range(10):
        out_ref[k] = near_ref[k]
        out_ref[10 + k] = second_ref[k]
        out_ref[20 + k] = third_ref[k]


def coarse_solve(mv, chip_ref, mine_ref, other_ref):
    window = []
    for w in range(WIN):
        rows = []
        ok = mv.marks[4 + w]
        for k in range(5):
            if w in (6, 7):
                rows.append(chip_ref[(w - 6) * 5 + k])
                continue
            if w < 6:
                slot = (2 - w // 2) * 10 + (w % 2) * 5 + k
                x = mv.pick(mine_ref[slot], other_ref[slot])
            else:
                slot = (w // 2 - 4) * 10 + (w % 2) * 5 + k
                x = mv.pick(other_ref[slot], mine_ref[slot])
            rows.append(x * ok)
        window.append(rows)
    coeffs = [rows[4] for rows in window]
    load, inverse, value = {}, {}, {}
    factor = COARSE_RELAX / (2.0 / 3.0)
    for j in range(2, 13):
        load[j] = [window[j - 1][2 + g] + window[j][g] for g in range(2)]
        k = coeffs[j - 1] + coeffs[j]
        k = k + mv.below(k)
        inverse[j] = [jnp.where(v > 0.0, factor / v, 0.0) for v in (k + mv.before(k), k)]
        value[j] = [inverse[j][g] * load[j][g] for g in range(2)]
    for step in range(NC - 1):
        first, final = 2 + step, 12 - step
        nodes = {}
        for j in range(first, final + 1):
            value[j][1] = mv.after(value[j][0], value[j][1])
            nodes[j] = [value[j], [mv.above(v) for v in value[j]]]
        sums = {j: [[None, None], [None, None]] for j in range(first, final + 1)}
        for j in range(first, final):
            v = {(a, b, c): nodes[j + b][a][c] for a in range(2) for b in range(2) for c in range(2)}
            for axis in range(3):
                v = butterfly(v, axis)
            cf = [coeffs[j] * 0.125, coeffs[j] * (0.125 * 2.0 / 3.0), coeffs[j] * (0.125 / 3.0)]
            v = {key: None if sum(key) == 0 else x * cf[sum(key) - 1] for key, x in v.items()}
            for axis in range(3):
                v = butterfly(v, axis)
            for (a, b, c), x in v.items():
                old = sums[j + b][a][c]
                sums[j + b][a][c] = x if old is None else old + x
        new = {}
        for j in range(first + 1, final):
            s = sums[j]
            row = [s[0][c] + mv.below(s[1][c]) for c in range(2)]
            row[0] = row[0] + mv.before(row[1])
            new[j] = [value[j][g] + inverse[j][g] * (load[j][g] - row[g]) for g in range(2)]
        value = new
    for j in value:
        value[j][1] = mv.after(value[j][0], value[j][1])
    lines = [[mv.pick(value[5 + m][g], value[6 + m][g]) for g in range(2)] for m in range(4)]
    return lines, mv.pick(coeffs[5], coeffs[6]), mv.pick(coeffs[7], coeffs[8])


def butterfly(v, axis):
    out = {}
    for key in v:
        if key[axis]:
            continue
        up = tuple(1 if k == axis else key[k] for k in range(3))
        x, y = v[key], v[up]
        out[key] = y if x is None else x + y
        out[up] = -y if x is None else x - y
    return out


def nodal(mv, pair, count):
    rows = []
    up = [mv.above(v) for v in pair]
    for a in range(count):
        lo, hi = float(INTERP[a, 0]), float(INTERP[a, 1])
        if a == 0:
            ends = pair
        elif a == 4:
            ends = up
        else:
            ends = [lo * pair[g] + hi * up[g] for g in range(2)]
        rows.append([ends[0] if c == 0 else ends[1] if c == 4 else float(INTERP[c, 0]) * ends[0] + float(INTERP[c, 1]) * ends[1] for c in range(N)])
    return rows


def neighbour_face(mv, near, far, coeff):
    w = [float(x) for x in weights]
    x = nodal(mv, near, N)
    z = nodal(mv, far, N)
    y = []
    for a in range(N):
        row = []
        for c in range(N):
            v = (x[a][c] - z[a][c]) * (0.5 * weight(a, c))
            if a in (0, 4):
                v = v + (x[a][c] - x[4 - a][c]) * (0.5 * w[0] * w[SYM[c]])
            if c in (0, 4):
                v = v + (x[a][c] - x[a][4 - c]) * (0.5 * w[0] * w[SYM[a]])
            row.append(v * coeff)
        y.append(row)
    out = []
    for a in range(4):
        row = [y[0][c] + mv.below(y[4][c]) for c in range(N)] if a == 0 else y[a]
        row[0] = row[0] + mv.before(row[4])
        out.extend(row)
    return out


def add_correction(mv, low, high, coeff, u_ref, y_ref, ua_ref, ya_ref):
    half = coeff * 0.5
    found = {}

    def v(a, b, c):
        if (a, b, c) not in found:
            lo, hi = low[a][c], high[a][c]
            found[a, b, c] = lo if b == 0 else hi if b == 4 else float(INTERP[b, 0]) * lo + float(INTERP[b, 1]) * hi
        return found[a, b, c]

    def share(a, b, c):
        parts = []
        if a in (0, 4):
            parts.append((v(a, b, c) - v(4 - a, b, c)) * weight(b, c))
        if b in (0, 4):
            parts.append((v(a, b, c) - v(a, 4 - b, c)) * weight(a, c))
        if c in (0, 4):
            parts.append((v(a, b, c) - v(a, b, 4 - c)) * weight(a, b))
        return sum(parts[1:], parts[0]) * half if parts else None

    for a in range(4):
        for b in range(N):
            row = [share(a, b, c) for c in range(N)]
            if a == 0:
                for c in range(N):
                    under = share(4, b, c)
                    row[c] = row[c] + mv.below(under)
            row[0] = row[0] + mv.before(row[4])
            for c in range(N):
                ua_ref[at(a, b, c)] = u_ref[at(a, b, c)] + v(a, b, c)
                ya_ref[at(a, b, c)] = y_ref[at(a, b, c)] if row[c] is None else y_ref[at(a, b, c)] + row[c]


def correct_kernel(marks, u_ref, y_ref, f_ref, inv_ref, coeff_ref, ga_ref, near_ref, chip_ref, mine_ref, other_ref, un_ref, yn_ref, a_ref, b_ref, ua_ref, ya_ref, face_ref, acc_ref, up_ref):
    mv = Moves(marks)
    coeff = coeff_ref[...]
    lines, coeff_left, coeff_right = coarse_solve(mv, chip_ref, mine_ref, other_ref)
    for k, v in enumerate(neighbour_face(mv, lines[1], lines[0], coeff_left)):
        face_ref[k] = v
    for k, v in enumerate(neighbour_face(mv, lines[2], lines[3], coeff_right)):
        face_ref[20 + k] = v
    low, high = nodal(mv, lines[1], N), nodal(mv, lines[2], N)
    add_correction(mv, low, high, coeff, u_ref, y_ref, ua_ref, ya_ref)
    left, right = got_faces(mv, ga_ref, near_ref, 17, 5, 10)
    left = [left[k] + face_ref[k] for k in range(20)]
    right = [right[k] + face_ref[20 + k] for k in range(20)]
    smooth(mv, ua_ref, f_ref, ya_ref, left, right, inv_ref, un_ref)
    apply_operator(mv, un_ref, coeff, yn_ref, acc_ref, up_ref)
    put_faces(mv, yn_ref, a_ref, b_ref)


def residual_kernel(marks, y_ref, f_ref, ga_ref, gb_ref, half_ref, r_ref):
    mv = Moves(marks)
    left, right = got_faces(mv, ga_ref, gb_ref, 17)
    for a in range(4):
        for b in range(N):
            r = residual_row(mv, f_ref, y_ref, left, right, a, b)
            r[4] = mv.after(r[0], r[4])
            for c in range(N):
                r_ref[at(a, b, c)] = r[c]
    half_rows(mv, r_ref, half_ref)


def spread_kernel(half_ref, out_ref):
    lane = lax.broadcasted_iota(jnp.int32, (8, 128), 1)
    ends = half_ref[pl.ds(320, 8)]
    for k in range(20):
        out_ref[pl.ds(20 * k, 16)] = half_ref[pl.ds(16 * k, 16)]
        last = jnp.where(lane == 127, pltpu.roll(ends, 127 - k, 1), pltpu.roll(half_ref[pl.ds(16 * k, 8)], 127, 1))
        out_ref[pl.ds(20 * k + 16, 4)] = last[:4]
    row = lax.broadcasted_iota(jnp.int32, (100, 128), 0)
    out_ref[pl.ds(400, 100)] = jnp.where((row & 3) == 3, 0.0, out_ref[pl.ds(1, 100)])


VM = pl.BlockSpec(memory_space=pltpu.VMEM)
FIELD = (100, 8, 128)
WORK = [(125, 8, 128), (25, 8, 128)]


def call(name, kernel, outs, scratch, *args, cost=None):
    return pl.pallas_call(
        kernel,
        out_shape=[jax.ShapeDtypeStruct(s, F32) for s in outs],
        in_specs=[VM] * len(args),
        out_specs=[VM] * len(outs),
        scratch_shapes=[pltpu.VMEM(s, F32) for s in scratch],
        compiler_params=pltpu.CompilerParams(vmem_limit_bytes=12 * 1024 * 1024),
        name=name,
        cost_estimate=cost,
    )(*args)


def placement(sizes):
    _, ey, lin = sizes
    place = list(range(ey * lin))
    if lin == 64:
        for s in place[:]:
            side, p, y, core = s // 64, s // 8 % 8, s // 2 % 4, s % 2
            z = (p - side) % 8
            place[s] = side * 64 + z * 8 + (3 - y if p % 2 else y) * 2 + core
    return place


def per_device(sizes):
    strips = sizes[1] * sizes[2]
    chips = strips // 2
    place = placement(sizes)
    device = [[copy * strips + place[s] for s in range(strips)] for copy in range(2)]
    to_same = [(e * strips + s, device[e][s]) for e in range(2) for s in range(strips)]
    to_other = [(e * strips + s, device[1 - e][s]) for e in range(2) for s in range(strips)]
    back = [(b, a) for a, b in to_same]
    within = [(device[e][s], device[e][s ^ 1]) for e in range(2) for s in range(strips)]

    def chip_pairs(d):
        pairs = []
        for e in range(2):
            for s in range(strips):
                k = s // 2 - d if s % 2 == 0 else s // 2 + d
                if 0 <= k < chips:
                    pairs.append((device[e][s], device[e][2 * k + 1 - s % 2]))
                else:
                    pairs.append((device[e][s], device[1 - e][s]))
        return pairs

    beyond = {d: chip_pairs(d) for d in (1, 2, 3)}
    table = np.zeros((2 * strips, 4 + WIN), np.float32)
    for copy in range(2):
        for s in range(strips):
            window = [0 <= s - s % 2 - 6 + w < strips for w in range(WIN)]
            table[device[copy][s]] = [s % 2 == 0, copy == 0, s > 0, s < strips - 1, *window]

    def swap(x, pairs):
        return lax.ppermute(x, AXES, pairs)

    def restore(x):
        return x if place == sorted(place) else swap(x, back)

    def run(load, kappa, wet):
        marks = lax.dynamic_index_in_dim(jnp.asarray(table), lax.axis_index(AXES), 0, keepdims=False)
        marks = jnp.broadcast_to(marks[:, None, None], (4 + WIN, 8, 128))
        coeff = kappa * jnp.where(wet == 1, 1.0, 0.05).astype(F32)
        packed = jnp.concatenate([load.reshape(500, 1, 128), coeff.reshape(4, 1, 128)]).reshape(504, 128)
        (packed,) = call("pack", pack_kernel, [(328, 128)], [(504, 128)], packed)
        same, other = packed if place == sorted(place) else swap(packed, to_same), swap(packed, to_other)
        part, coeff, a, b = call("unpack", unpack_kernel, [FIELD, (8, 128), (18, 8, 128), (18, 8, 128)], [], marks, same, other)
        faces = [(17, 8, 128), (17, 8, 128)]

        def trade(a, b):
            return swap(a, within), swap(b, beyond[1])

        a, b = trade(a, b)
        u, y, f, inv, a, b = call("first", first_kernel, [FIELD, FIELD, FIELD, (12, 8, 128), *faces], WORK, marks, part, coeff, a, b)

        def inner(u, y):
            cost = pl.CostEstimate(flops=2000000, bytes_accessed=1500000, transcendentals=0)
            return call("inner", inner_kernel, [FIELD, (125, 8, 128)], [], u, y, f, inv, cost=cost)

        def sweep(u, y, a, b):
            a, b = trade(a, b)
            return call("sweep", sweep_kernel, [FIELD, FIELD, *faces], WORK, marks, u, y, f, inv, coeff, *inner(u, y), a, b)

        def sweep_and_correct(u, y, a, b):
            a, b = trade(a, b)
            u, y, own, a, b = call("restrict", restrict_kernel, [FIELD, FIELD, (5, 8, 128), (22, 8, 128), (22, 8, 128)], WORK, marks, u, y, f, inv, coeff, *inner(u, y), a, b, part)
            a = swap(a, within)
            chip, near = call("chip", chip_kernel, [(10, 8, 128), (27, 8, 128)], [], marks, own, a, b)
            near, second, third = swap(near, beyond[1]), swap(chip, beyond[2]), swap(chip, beyond[3])
            (mine,) = call("side", side_kernel, [(30, 8, 128)], [], near, second, third)
            theirs = swap(mine, within)
            return call("correct", correct_kernel, [FIELD, FIELD, *faces], [FIELD, FIELD, (40, 8, 128), *WORK], marks, u, y, f, inv, coeff, a, near, chip, mine, theirs)

        u, y, a, b = sweep_and_correct(u, y, a, b)
        u, y, a, b = sweep(u, y, a, b)
        u, y, a, b = sweep(u, y, a, b)
        u, y, a, b = sweep_and_correct(u, y, a, b)
        a, b = trade(a, b)
        y, a, b, half = call("last", last_sweep_kernel, [FIELD, *faces, (328, 128)], [FIELD, *WORK], marks, u, y, f, inv, coeff, *inner(u, y), a, b)
        a, b = trade(a, b)
        a, b, half = lax.optimization_barrier((a, b, half))
        half = restore(half)
        (left_half,) = call("residual", residual_kernel, [(328, 128)], [FIELD], marks, y, f, a, b)
        (solved,) = call("spread", spread_kernel, [(500, 128)], [], half)
        (rest,) = call("spread", spread_kernel, [(500, 128)], [], restore(left_half))
        return solved.reshape(load.shape), rest.reshape(load.shape)

    return run


def solution(mesh):
    sizes = tuple(mesh.shape[name] for name in AXES)
    whole = P(None, None, None, None, ("ey", "lin"), "ex")
    flat = P(None, ("ey", "lin"), "ex")
    return jax.shard_map(per_device(sizes), mesh=mesh, in_specs=(whole, flat, flat), out_specs=(whole, whole), check_vma=False)
```
